768 devices in a mesh: grp: 48 (over z, x), mem: 16 (over y, core).
Axes of the slice: x: 4, y: 8, z: 12, core: 2. Of those that a mesh axis runs over, the one named last changes fastest.
Arguments:
- source_rows: bfloat16 [393216, 256], P(('grp', 'mem')), may hold values from -6 to 6
- source_degree: int32 [393216], P(('grp', 'mem')), may hold values from 1 to 32
- edge_tiles: int32 [24576, 128, 128], P(('grp', 'mem')), may hold values 0 or 1
- tile_row: int32 [24576], P(('grp', 'mem')), may hold values from 0 to 7
- tile_col: int32 [24576], P(('grp', 'mem')), may hold values from 0 to 3
- mirror_ids: int32 [786432], P(('grp', 'mem')), may hold values from 0 to 24575, as said below
- master_rows: bfloat16 [24576, 256], P(('grp', 'mem')), may hold values from -6 to 6
- master_degree: int32 [24576], P(('grp', 'mem')), may hold values from 64 to 1024
- weight_one: bfloat16 [256, 256], replicated, may hold values from -0.375 to 0.375
- weight_two: bfloat16 [256, 256], replicated, may hold values from -0.375 to 0.375
Outputs:
- new_master: bfloat16 [24576, 256], P(('grp', 'mem'))
- mirror_out: bfloat16 [786432, 256], P(('grp', 'mem'))
The draws below stay inside these ranges and needn't reach their ends.
Inputs may be any that keep to these rules, and one draw needn't show every extreme that they name: `mirror_ids`: entry j of a device's 1024 entries names a vertex whose owning device has mem index j // 64; vertex v is owned by device v // 32, devices counted grp first then mem.
All inputs are finite; a program needn't handle non-finite values. No bound on the sum of `edge_tiles` on one device may be relied on, other than what follows from the above.
Results may differ from the reference program's by a relative error of at most 0.0053.
Values may be sent and summed in bfloat16 or wider, within the bound.
A program may use at most 32 MiB of HBM per device.

```python
import jax
import jax.numpy as jnp
from jax import lax

D = 256
TILE = 128
TILES_DEV = 32
SRC_DEV = 512
SLOTS = 64
MASTER_DEV = 32
DEVICES_ALL = 768
VERTICES = 24576
N_GRP = 48
N_MEM = 16


def draw_mirror_ids(key, part):
    key = jax.random.fold_in(key, 7)
    key_one, key_two, key_three = jax.random.split(key, 3)
    shape_all = (N_GRP * N_MEM, N_MEM, SLOTS)
    first_group = jax.random.randint(key_one, shape_all, 0, N_GRP)
    second_group = jax.random.randint(key_two, shape_all, 0, N_GRP)
    group_pick = jnp.minimum(first_group, second_group)
    offset = jax.random.randint(key_three, shape_all, 0, MASTER_DEV)
    member = jnp.arange(N_MEM, dtype=jnp.int32)[None, :, None]
    flat = ((group_pick * N_MEM + member) * MASTER_DEV + offset).reshape(-1).astype(jnp.int32)
    flat = flat.at[0].set(jnp.int32(0))
    flat = flat.at[-1].set(jnp.int32(MASTER_DEV * N_GRP * N_MEM - 1))
    return flat


def touch_ends(drawn, key, least, top_value):
    spot = [jax.random.randint(jax.random.fold_in(key, axis), (), 0, length) for axis, length in enumerate(drawn.shape)]
    main_axis = drawn.shape.index(max(drawn.shape))
    next_to = spot[:main_axis] + [(spot[main_axis] + 1) % drawn.shape[main_axis]] + spot[main_axis + 1:]
    return drawn.at[tuple(spot)].set(least).at[tuple(next_to)].set(top_value)


def steps_of(rng, dims, cuts, smallest, top_value):
    level, own = 1.0, jax.random.fold_in(rng, 6)
    for position, blocks in cuts:
        draws = jnp.exp(jax.random.uniform(jax.random.fold_in(own, position), (blocks,), jnp.float32, smallest / len(cuts), top_value / len(cuts)))
        level = level * jnp.repeat(draws, dims[position] // blocks).reshape([-1 if axis == position else 1 for axis in range(len(dims))])
    return level


def centred(stream_key, extent, deviation, reach, cuts=(), kind=jnp.bfloat16):
    drawn = deviation * jax.random.normal(stream_key, extent, jnp.float32)
    if cuts:
        drawn = drawn * steps_of(stream_key, extent, cuts, -0.22, 0.18)
    return jnp.clip(drawn, -reach, reach).astype(kind)


def setup_inputs(seed: int = 0) -> dict:
    splits = jax.random.split(jax.random.key(seed), 11)
    source_rows = centred(splits[0], (DEVICES_ALL * SRC_DEV, D), 1.0, 6.0, ((0, 768),))
    source_degree = touch_ends(jax.random.randint(splits[1], (DEVICES_ALL * SRC_DEV,), 1, 33), jax.random.fold_in(splits[1], 1), 1, 32).astype(jnp.int32)
    edge_tiles = touch_ends((jax.random.randint(splits[2], (DEVICES_ALL * TILES_DEV, TILE, TILE), 0, 16) < 1).astype(jnp.int32), jax.random.fold_in(splits[2], 1), 0, 1)
    tile_row = touch_ends(jax.random.randint(splits[3], (DEVICES_ALL * TILES_DEV,), 0, N_MEM * SLOTS // TILE), jax.random.fold_in(splits[3], 1), 0, (N_MEM * SLOTS // TILE) - 1).astype(jnp.int32)
    tile_col = touch_ends(jax.random.randint(splits[4], (DEVICES_ALL * TILES_DEV,), 0, SRC_DEV // TILE), jax.random.fold_in(splits[4], 1), 0, (SRC_DEV // TILE) - 1).astype(jnp.int32)
    mirror_ids = draw_mirror_ids(jax.random.fold_in(splits[10], 71), 0)
    master_rows = centred(splits[6], (VERTICES, D), 1.0, 6.0, ((0, 768),))
    master_degree = touch_ends(jax.random.randint(splits[7], (VERTICES,), 64, 1025), jax.random.fold_in(splits[7], 1), 64, 1024).astype(jnp.int32)
    weight_one = centred(splits[8], (D, D), D ** -0.5, 0.375)
    weight_two = centred(splits[9], (D, D), D ** -0.5, 0.375)
    return {"source_rows": source_rows, "source_degree": source_degree, "edge_tiles": edge_tiles, "tile_row": tile_row, "tile_col": tile_col, "mirror_ids": mirror_ids, "master_rows": master_rows, "master_degree": master_degree, "weight_one": weight_one, "weight_two": weight_two}


def update_rows(summed, rows_in, degree, weight_one, weight_two):
    neigh = summed * lax.rsqrt(degree.astype(jnp.float32))[:, None]
    embed = rows_in.astype(jnp.float32)
    first = (embed + neigh).astype(jnp.bfloat16)
    second = (neigh * embed).astype(jnp.bfloat16)
    result = jnp.dot(first, weight_one, preferred_element_type=jnp.float32) + jnp.dot(second, weight_two, preferred_element_type=jnp.float32)
    return jnp.where(result > 0, result, 0.2 * result).astype(jnp.bfloat16)

def reference(source_rows, source_degree, edge_tiles, tile_row, tile_col, mirror_ids, master_rows, master_degree, weight_one, weight_two):
    device_count = N_GRP * N_MEM
    mirror_count = N_MEM * SLOTS
    scaled = (source_rows.astype(jnp.float32) * lax.rsqrt(source_degree.astype(jnp.float32))[:, None]).astype(jnp.bfloat16)
    vertex_count = MASTER_DEV * device_count

    def one_device(total, inputs):
        held_rows, tiles_here, rows_here, cols_here, ids_here = inputs
        blocks = held_rows.reshape(-1, TILE, D)
        picked = blocks[cols_here].astype(jnp.float32)
        products = jnp.einsum('trc,tcd->trd', tiles_here.astype(jnp.float32), picked, precision=lax.Precision.HIGHEST)
        onehot = (rows_here[:, None] == jnp.arange(mirror_count // TILE, dtype=jnp.int32)[None, :]).astype(jnp.float32)
        partial_value = jnp.einsum('tb,trd->brd', onehot, products, precision=lax.Precision.HIGHEST).reshape(mirror_count, D)
        return (total.at[ids_here].add(partial_value), None)
    total, _ = lax.scan(one_device, jnp.zeros((vertex_count, D), jnp.float32), (scaled.reshape(device_count, SRC_DEV, D), edge_tiles.reshape(device_count, TILES_DEV, TILE, TILE), tile_row.reshape(device_count, TILES_DEV), tile_col.reshape(device_count, TILES_DEV), mirror_ids.reshape(device_count, mirror_count)))
    new_master = update_rows(total, master_rows, master_degree, weight_one, weight_two)
    mirror_out = new_master[mirror_ids]
    return (new_master, mirror_out)
```

```python
import functools

import jax
import jax.numpy as jnp
from jax import lax
from jax.experimental import pallas as pl
from jax.experimental.pallas import tpu as pltpu
from jax.sharding import PartitionSpec as P

MESH = pl.DeviceIdType.MESH
NX = 4
LANE = 128
HALVES = 2


def local_kernel(trow, tcol, src, deg, tiles, out, scaled, acc):
    tile = tiles.shape[1]
    n_tiles = tiles.shape[0]
    scale = lax.rsqrt(deg[...].astype(jnp.float32))
    for k in range(src.shape[0] // tile):
        column = jnp.broadcast_to(scale[k : k + 1, :], (tile, tile)).T
        rows = pl.ds(k * tile, tile)
        for h in range(HALVES):
            cols = pl.ds(h * LANE, LANE)
            scaled[rows, cols] = (src[rows, cols].astype(jnp.float32) * column).astype(jnp.bfloat16)
    acc[...] = jnp.zeros_like(acc)

    def one(t, carry):
        r = pl.multiple_of(trow[t] * tile, tile)
        c = pl.multiple_of(tcol[t] * tile, tile)
        edges = tiles[t].astype(jnp.float32).astype(jnp.bfloat16)
        acc[pl.ds(r, tile), :] += jnp.dot(
            edges, scaled[pl.ds(c, tile), :], preferred_element_type=jnp.float32
        )
        return carry

    lax.fori_loop(0, n_tiles, one, 0, unroll=4)
    for h in range(HALVES):
        out[h] = acc[:, h * LANE : (h + 1) * LANE].astype(jnp.bfloat16)


def exchange_kernel(
    n_grp, n_mem, part, ids, mrow, mdeg, w1, w2, newm, mirror,
    precv, idrecv, idrow, put, take, col, xacc, xrecv, zsend, zrecv, colnew, served,
    id_s, id_r, y_s, y_r, x_s, x_r, z_s, z_r, gz_s, gz_r, gx_s, gx_r, b_s, b_r,
):
    g = lax.axis_index("grp")
    m = lax.axis_index("mem")
    n_z = n_grp // NX
    x = lax.rem(g, NX)
    z = g // NX
    slots = part.shape[1] // n_mem
    owned = mrow.shape[0]
    xrows = n_z * owned

    def at_mem(k):
        return lax.rem(m + k, n_mem)

    def at_x(k):
        return lax.rem(x + k, NX)

    def at_z(k):
        return lax.rem(z + k, n_z)

    barrier = pltpu.get_barrier_semaphore()

    def hello_mem(k, carry):
        pl.semaphore_signal(barrier, inc=1, device_id=(g, at_mem(k)), device_id_type=MESH)
        return carry

    def hello_x(k, carry):
        pl.semaphore_signal(barrier, inc=1, device_id=(z * NX + at_x(k), m), device_id_type=MESH)
        return carry

    def hello_z(k, carry):
        pl.semaphore_signal(barrier, inc=1, device_id=(at_z(k) * NX + x, m), device_id_type=MESH)
        return carry

    lax.fori_loop(1, n_mem, hello_mem, 0)
    lax.fori_loop(1, NX, hello_x, 0)
    lax.fori_loop(1, n_z, hello_z, 0)
    pl.semaphore_wait(barrier, (n_mem - 1) + (NX - 1) + (n_z - 1))

    def each(count, fn):
        def body(k, carry):
            fn(k)
            return carry

        lax.fori_loop(1, count, body, 0)

    def id_copy(to, who):
        return pltpu.make_async_remote_copy(
            src_ref=ids.at[to], dst_ref=idrecv.at[who], send_sem=id_s.at[to], recv_sem=id_r.at[who],
            device_id=(g, to), device_id_type=MESH)

    def y_copy(h, to, who):
        return pltpu.make_async_remote_copy(
            src_ref=part.at[h, pl.ds(to * slots, slots)], dst_ref=precv.at[h, pl.ds(who * slots, slots)],
            send_sem=y_s.at[h, to], recv_sem=y_r.at[h, who], device_id=(g, to), device_id_type=MESH)

    def x_copy(h, to, who):
        return pltpu.make_async_remote_copy(
            src_ref=col.at[h, to], dst_ref=xrecv.at[h, who], send_sem=x_s.at[h, to], recv_sem=x_r.at[h, who],
            device_id=(z * NX + to, m), device_id_type=MESH)

    def z_copy(h, to, who):
        return pltpu.make_async_remote_copy(
            src_ref=zsend.at[h, pl.ds(to * owned, owned)], dst_ref=zrecv.at[h, who],
            send_sem=z_s.at[h, to], recv_sem=z_r.at[h, who], device_id=(to * NX + x, m), device_id_type=MESH)

    def gz_copy(to, who):
        block = colnew.at[:, x, pl.ds(who * owned, owned)]
        return pltpu.make_async_remote_copy(
            src_ref=block, dst_ref=block, send_sem=gz_s.at[to], recv_sem=gz_r.at[who],
            device_id=(to * NX + x, m), device_id_type=MESH)

    def gx_copy(h, to, who):
        block = colnew.at[h, who]
        return pltpu.make_async_remote_copy(
            src_ref=block, dst_ref=block, send_sem=gx_s.at[h, to], recv_sem=gx_r.at[h, who],
            device_id=(z * NX + to, m), device_id_type=MESH)

    def b_copy(h, to, who):
        return pltpu.make_async_remote_copy(
            src_ref=served.at[h, pl.ds(to * slots, slots)],
            dst_ref=mirror.at[pl.ds(who * slots, slots), pl.ds(h * LANE, LANE)],
            send_sem=b_s.at[h, to], recv_sem=b_r.at[h, who], device_id=(g, to), device_id_type=MESH)

    each(n_mem, lambda k: id_copy(at_mem(k), m).start())
    for h in range(HALVES):
        each(n_mem, lambda k: y_copy(h, at_mem(k), m).start())
    idrecv[m] = ids[m]
    mine = pl.ds(pl.multiple_of(m * slots, slots), slots)
    for h in range(HALVES):
        precv[h, mine, :] = part[h, mine, :]
    each(n_mem, lambda k: id_copy(m, at_mem(k)).wait_recv())

    for k in range(n_mem * slots // LANE):
        lane = lax.broadcasted_iota(jnp.int32, (8, LANE), 1)
        idrow[:, k * LANE : (k + 1) * LANE] = jnp.where(lane < slots, idrecv[2 * k], idrecv[2 * k + 1])

    def build_put(q, carry):
        rows = lax.broadcasted_iota(jnp.int32, (LANE, n_mem * slots), 0) + q * LANE
        put[pl.ds(pl.multiple_of(q * LANE, LANE), LANE), :] = jnp.where(
            rows == idrow[0:1, :], 1.0, 0.0).astype(jnp.bfloat16)
        return carry

    lax.fori_loop(0, NX * xrows // LANE, build_put, 0)

    def build_take(k, carry):
        at = pl.ds(pl.multiple_of(k * LANE, LANE), LANE)
        column = jnp.broadcast_to(idrow[0:1, at], (LANE, LANE)).T
        for q in range(NX * xrows // LANE):
            lane = lax.broadcasted_iota(jnp.int32, (LANE, LANE), 1) + q * LANE
            take[at, q * LANE : (q + 1) * LANE] = jnp.where(column == lane, 1.0, 0.0).astype(jnp.bfloat16)
        return carry

    for h in range(HALVES):
        each(n_mem, lambda k: y_copy(h, m, at_mem(k)).wait_recv())
        for k in (2, 1, 3, 0):
            to = at_x(k)
            block = jnp.dot(
                put[pl.ds(pl.multiple_of(to * xrows, xrows), xrows), :], precv[h],
                preferred_element_type=jnp.float32)
            if k:
                col[h, to] = block.astype(jnp.bfloat16)
                x_copy(h, to, x).start()
            else:
                xacc[h] = block
    lax.fori_loop(0, n_mem * slots // LANE, build_take, 0)

    for h in range(HALVES):
        each(NX, lambda k: x_copy(h, x, at_x(k)).wait_recv())
        total = xacc[h]
        for k in range(1, NX):
            total = total + xrecv[h, at_x(k)].astype(jnp.float32)
        xacc[h] = total
        zsend[h] = total.astype(jnp.bfloat16)
        each(n_z, lambda k: z_copy(h, at_z(k), z).start())

    own = pl.ds(pl.multiple_of(z * owned, owned), owned)
    sums = []
    for h in range(HALVES):
        zrecv[h, z] = jnp.zeros((owned, LANE), jnp.bfloat16)
        each(n_z, lambda k: z_copy(h, z, at_z(k)).wait_recv())
        total = xacc[h, own, :]
        for k in range(n_z):
            total = total + zrecv[h, k].astype(jnp.float32)
        sums.append(total)

    scale = lax.rsqrt(mdeg[...].astype(jnp.float32))
    diagonal = lax.broadcasted_iota(jnp.int32, (owned, owned), 0) == lax.broadcasted_iota(
        jnp.int32, (owned, owned), 1)
    scale = jnp.sum(jnp.where(diagonal, jnp.broadcast_to(scale, (owned, owned)), 0.0), axis=1, keepdims=True)
    neigh = jnp.concatenate(sums, axis=1) * scale
    embed = mrow[...].astype(jnp.float32)
    first = (embed + neigh).astype(jnp.bfloat16)
    second = (neigh * embed).astype(jnp.bfloat16)
    result = jnp.dot(first, w1[...], preferred_element_type=jnp.float32) + jnp.dot(
        second, w2[...], preferred_element_type=jnp.float32)
    new = jnp.where(result > 0, result, 0.2 * result).astype(jnp.bfloat16)
    newm[...] = new
    for h in range(HALVES):
        colnew[h, x, own, :] = new[:, h * LANE : (h + 1) * LANE]

    each(n_z, lambda k: gz_copy(at_z(k), z).start())
    each(n_z, lambda k: gz_copy(z, at_z(k)).wait_recv())
    for h in range(HALVES):
        for k in (2, 1, 3):
            gx_copy(h, at_x(k), x).start()
    for h in range(HALVES):
        each(NX, lambda k: gx_copy(h, x, at_x(k)).wait_recv())
        table = colnew[h].reshape(NX * xrows, LANE)
        served[h] = jnp.dot(take[...], table, preferred_element_type=jnp.float32).astype(jnp.bfloat16)
        each(n_mem, lambda k: b_copy(h, at_mem(k), m).start())
        mirror[mine, h * LANE : (h + 1) * LANE] = served[h, mine, :]

    each(n_mem, lambda k: id_copy(at_mem(k), m).wait_send())
    for h in range(HALVES):
        each(n_mem, lambda k: y_copy(h, at_mem(k), m).wait_send())
        each(NX, lambda k: x_copy(h, at_x(k), x).wait_send())
        each(n_z, lambda k: z_copy(h, at_z(k), z).wait_send())
        each(NX, lambda k: gx_copy(h, at_x(k), x).wait_send())
    each(n_z, lambda k: gz_copy(at_z(k), z).wait_send())
    for h in range(HALVES):
        each(n_mem, lambda k: b_copy(h, m, at_mem(k)).wait_recv())
        each(n_mem, lambda k: b_copy(h, at_mem(k), m).wait_send())


def body(n_grp, n_mem, source_rows, source_degree, edge_tiles, tile_row, tile_col, mirror_ids,
         master_rows, master_degree, weight_one, weight_two):
    n_tiles, tile, _ = edge_tiles.shape
    src_dev, width = source_rows.shape
    slot_total = mirror_ids.shape[0]
    slots = slot_total // n_mem
    owned = master_rows.shape[0]
    n_z = n_grp // NX
    xrows = n_z * owned
    vmem = pl.BlockSpec(memory_space=pltpu.VMEM)
    smem = pl.BlockSpec(memory_space=pltpu.SMEM)
    bf, f32, i32 = jnp.bfloat16, jnp.float32, jnp.int32

    part = pl.pallas_call(
        local_kernel,
        out_shape=jax.ShapeDtypeStruct((HALVES, slot_total, LANE), bf),
        in_specs=[smem, smem, vmem, vmem, vmem],
        out_specs=vmem,
        scratch_shapes=[pltpu.VMEM((src_dev, width), bf), pltpu.VMEM((slot_total, width), f32)],
        compiler_params=pltpu.CompilerParams(vmem_limit_bytes=24 * 2**20),
        name="local_sums",
    )(tile_row, tile_col, source_rows, source_degree.reshape(-1, tile), edge_tiles)

    group = mirror_ids // (owned * n_mem)
    place = lax.rem(group, NX) * xrows + (group // NX) * owned + lax.rem(mirror_ids, owned)
    place = place.reshape(n_mem, 1, slots)
    ids = jnp.broadcast_to(jnp.concatenate([place, place], axis=2), (n_mem, 8, 2 * slots))

    dma = pltpu.SemaphoreType.DMA
    return pl.pallas_call(
        functools.partial(exchange_kernel, n_grp, n_mem),
        out_shape=(
            jax.ShapeDtypeStruct((owned, width), bf),
            jax.ShapeDtypeStruct((slot_total, width), bf),
        ),
        in_specs=[vmem] * 6,
        out_specs=(vmem, vmem),
        scratch_shapes=[
            pltpu.VMEM((HALVES, slot_total, LANE), bf),
            pltpu.VMEM((n_mem, 8, LANE), i32),
            pltpu.VMEM((8, slot_total), i32),
            pltpu.VMEM((NX * xrows, slot_total), bf),
            pltpu.VMEM((slot_total, NX * xrows), bf),
            pltpu.VMEM((HALVES, NX, xrows, LANE), bf),
            pltpu.VMEM((HALVES, xrows, LANE), f32),
            pltpu.VMEM((HALVES, NX, xrows, LANE), bf),
            pltpu.VMEM((HALVES, xrows, LANE), bf),
            pltpu.VMEM((HALVES, n_z, owned, LANE), bf),
            pltpu.VMEM((HALVES, NX, xrows, LANE), bf),
            pltpu.VMEM((HALVES, slot_total, LANE), bf),
            dma((n_mem,)), dma((n_mem,)),
            dma((HALVES, n_mem)), dma((HALVES, n_mem)),
            dma((HALVES, NX)), dma((HALVES, NX)),
            dma((HALVES, n_z)), dma((HALVES, n_z)),
            dma((n_z,)), dma((n_z,)),
            dma((HALVES, NX)), dma((HALVES, NX)),
            dma((HALVES, n_mem)), dma((HALVES, n_mem)),
        ],
        compiler_params=pltpu.CompilerParams(
            collective_id=0, has_side_effects=True, vmem_limit_bytes=40 * 2**20),
        name="exchange",
    )(part, ids, master_rows, master_degree.reshape(1, owned), weight_one, weight_two)


def solution(mesh):
    both = ("grp", "mem")
    in_specs = (
        P(both, None), P(both), P(both, None, None), P(both), P(both), P(both),
        P(both, None), P(both), P(), P(),
    )
    out_specs = (P(both, None), P(both, None))
    fn = functools.partial(body, mesh.shape["grp"], mesh.shape["mem"])
    return jax.shard_map(fn, mesh=mesh, in_specs=in_specs, out_specs=out_specs, check_vma=False)
```

```python
import functools

import jax
import jax.numpy as jnp
from jax import lax
from jax.experimental import pallas as pl
from jax.experimental.pallas import tpu as pltpu
from jax.sharding import PartitionSpec as P

MESH = pl.DeviceIdType.MESH
NX = 4
NC = 2
LANE = 128
HALVES = 2
PARTS = 3
FETCH = 4


def log2(n):
    assert n & (n - 1) == 0
    return n.bit_length() - 1


def kernel(
    n_grp, n_mem, trow_h, tcol_h, src_h, deg_h, tiles_h, ids_h, mrow_h, mdeg_h, w1_h, w2_h, newm, mirror,
    trow, tcol, src, deg, tiles, idin, mrow, mdeg, w1, w2,
    scaled, bits, lhs, rhs, part, place, idrecv, even, odd, put, take, precv, col, xacc, xrecv, zsend, zrecv, table, served,
    newv, out_s, in_s, tile_s, id_s, id_r, y_s, y_r, x_s, x_r, z_s, z_r, gz_s, gz_r, gx_s, gx_r, b_s, b_r,
):
    g = lax.axis_index("grp")
    m = lax.axis_index("mem")
    n_z, n_y = n_grp // NX, n_mem // NC
    x, z = lax.rem(g, NX), g // NX
    c, y = lax.rem(m, NC), m // NC
    tile = tiles.shape[1]
    n_tiles = tiles.shape[0]
    slot_total = precv.shape[1]
    slots = slot_total // n_mem
    owned = mrow.shape[0]
    half_z = n_z // 2
    z_part = n_z // PARTS
    rows = z_part * owned

    def mem_of(dy, dc):
        return lax.rem(y + dy + n_y, n_y) * NC + lax.rem(c + dc, NC)

    def grp_x(j):
        return z * NX + lax.rem(x + j + NX, NX)

    def grp_z(k):
        return lax.rem(z + k + n_z, n_z) * NX + x

    def pos(k):
        return 2 * abs(k - half_z) - (1 if k < half_z else 0)

    y_order = [0] + [s for d in range(1, n_y // 2) for s in (n_y - d, d)] + [n_y // 2]
    mem_order = [(dy, dc) for dy in reversed(y_order) for dc in range(NC) if (dy, dc) != (0, 0)]
    x_order = sorted(range(1, NX), key=lambda j: -min(j, NX - j))
    z_order = sorted(range(1, n_z), key=pos)

    fetch = [
        pltpu.make_async_copy(a, b, in_s.at[i])
        for i, (a, b) in enumerate([
            (deg_h, deg), (src_h, src), (trow_h, trow), (tcol_h, tcol), (ids_h, idin),
            (mrow_h, mrow), (mdeg_h, mdeg), (w1_h, w1), (w2_h, w2)])
    ]
    step = n_tiles // FETCH
    fetch_tiles = [
        pltpu.make_async_copy(tiles_h.at[pl.ds(i * step, step)], tiles.at[pl.ds(i * step, step)], tile_s.at[i])
        for i in range(FETCH)
    ]
    for copy in fetch[:5]:
        copy.start()
    for copy in fetch_tiles:
        copy.start()
    for copy in fetch[5:]:
        copy.start()

    barrier = pltpu.get_barrier_semaphore()
    partners = [(grp_z(k), m) for k in z_order] + [(g, mem_of(*d)) for d in mem_order] + [
        (grp_x(j), m) for j in x_order]
    for who in partners:
        pl.semaphore_signal(barrier, inc=1, device_id=who, device_id_type=MESH)

    fetch[0].wait()
    fetch[1].wait()
    scale = lax.rsqrt(deg[...].astype(jnp.float32))
    for k in range(src.shape[0] // tile):
        column = jnp.broadcast_to(scale[k : k + 1, :], (tile, tile)).T
        for h in range(HALVES):
            at = (pl.ds(k * tile, tile), pl.ds(h * LANE, LANE))
            scaled[h, k] = (src[at].astype(jnp.float32) * column).astype(jnp.bfloat16)
    for copy in fetch[2:5]:
        copy.wait()

    ids = idin[...]
    group = jnp.right_shift(ids, log2(owned * n_mem))
    dx = jnp.bitwise_and(group, NX - 1) - x
    dx = jnp.where(dx < 0, dx + NX, dx)
    dz = jnp.right_shift(group, log2(NX)) - z
    dz = jnp.where(dz < 0, dz + n_z, dz)
    order = 2 * jnp.abs(dz - half_z) - jnp.where(dz < half_z, 1, 0)
    z_group = jnp.right_shift(order, log2(z_part))
    spots = (z_group * NX + dx) * rows + jnp.bitwise_and(order, z_part - 1) * owned + jnp.bitwise_and(
        ids, owned - 1)

    for k in range(n_y):
        place[k] = spots[k : k + 1, :]

    for i in range(FETCH):
        fetch_tiles[i].wait()
        for t in range(i * step, (i + 1) * step):
            bits[t] = tiles[t].astype(jnp.float32).astype(jnp.bfloat16)

    def sums_for(h, dy):
        block = lax.rem(y + dy, n_y)
        if h == 0:
            for t in range(n_tiles):
                edges = bits[t]
                lhs[dy, :, t * tile : (t + 1) * tile] = jnp.where(trow[t] == block, edges, jnp.zeros_like(edges))
        part[h, dy] = jnp.dot(lhs[dy], rhs[h], preferred_element_type=jnp.float32).astype(jnp.bfloat16)


    def slot_of(dy, dc):
        return dy * NC + dc

    def id_copy(dy, dc):
        return pltpu.make_async_remote_copy(
            src_ref=place.at[lax.rem(y + dy, n_y)], dst_ref=idrecv.at[slot_of(dy, dc)], send_sem=id_s, recv_sem=id_r,
            device_id=(g, mem_of(dy, dc)), device_id_type=MESH)

    def y_copy(h, dy, dc):
        to = mem_of(dy, dc)
        return pltpu.make_async_remote_copy(
            src_ref=part.at[h, dy, pl.ds(pl.multiple_of(lax.rem(to, NC) * slots, slots), slots)],
            dst_ref=precv.at[h, pl.ds(slot_of(dy, dc) * slots, slots)],
            send_sem=y_s.at[h], recv_sem=y_r.at[h], device_id=(g, to), device_id_type=MESH)

    def x_copy(h, q, j):
        return pltpu.make_async_remote_copy(
            src_ref=col.at[h, q, j], dst_ref=xrecv.at[h, q, j], send_sem=x_s.at[h], recv_sem=x_r.at[h, q],
            device_id=(grp_x(j), m), device_id_type=MESH)

    def z_copy(h, k):
        return pltpu.make_async_remote_copy(
            src_ref=zsend.at[h, pos(k)], dst_ref=zrecv.at[h, k], send_sem=z_s.at[h], recv_sem=z_r.at[h],
            device_id=(grp_z(k), m), device_id_type=MESH)

    def z_rows(k):
        return pos(k) // z_part, pl.ds(pos(k) % z_part * owned, owned)

    def gz_copy(h, k):
        q, at = z_rows(0)
        to_q, to_at = z_rows((n_z - k) % n_z)
        return pltpu.make_async_remote_copy(
            src_ref=table.at[h, q, 0, at], dst_ref=table.at[h, to_q, 0, to_at], send_sem=gz_s,
            recv_sem=gz_r.at[h, to_q], device_id=(grp_z(k), m), device_id_type=MESH)

    def gx_copy(h, q, j):
        return pltpu.make_async_remote_copy(
            src_ref=table.at[h, q, 0], dst_ref=table.at[h, q, NX - j], send_sem=gx_s.at[h], recv_sem=gx_r.at[h],
            device_id=(grp_x(j), m), device_id_type=MESH)

    def b_copy(h, dy, dc):
        to = mem_of(-dy, dc)
        return pltpu.make_async_remote_copy(
            src_ref=served.at[h, pl.ds(slot_of(dy, dc) * slots, slots)],
            dst_ref=mirror.at[pl.ds(pl.multiple_of(m * slots, slots), slots), pl.ds(h * LANE, LANE)],
            send_sem=b_s.at[h], recv_sem=b_r.at[h], device_id=(g, to), device_id_type=MESH)

    def drain(ref, sem):
        pltpu.make_async_copy(ref, ref, sem).wait()

    mine = pl.ds(pl.multiple_of(m * slots, slots), slots)
    idrecv[0] = place[y]
    for h in range(HALVES):
        for t in range(n_tiles):
            rhs[h, t * tile : (t + 1) * tile, :] = scaled[h, tcol[t]]
        for i, dy in enumerate(reversed(y_order)):
            sums_for(h, dy)
            if h == 0 and i == 0:
                pl.semaphore_wait(barrier, len(partners))
                for d in mem_order:
                    id_copy(*d).start()
            for dc in range(NC):
                if (dy, dc) != (0, 0):
                    y_copy(h, dy, dc).start()
        precv[h, 0:slots] = part[h, 0, pl.ds(pl.multiple_of(c * slots, slots), slots), :]

    drain(idrecv.at[pl.ds(1, n_mem - 1)], id_r)
    for k in range(n_y):
        even[k : k + 1, :] = idrecv[NC * k]
        odd[k : k + 1, :] = idrecv[NC * k + 1]
    lane = lax.broadcasted_iota(jnp.int32, (n_y, LANE), 1)
    low = jnp.where(c == 0, even[...], pltpu.roll(even[...], slots, 1))
    high = jnp.where(c == 0, pltpu.roll(odd[...], slots, 1), odd[...])
    spot = jnp.where(lane < slots, low, high)
    n_table = PARTS * NX * rows
    even[...] = spot

    def build_put(v, carry):
        row = lax.broadcasted_iota(jnp.int32, (LANE, LANE), 0) + v * LANE
        for k in range(n_y):
            put[pl.ds(pl.multiple_of(v * LANE, LANE), LANE), k * LANE : (k + 1) * LANE] = jnp.where(
                row == even[k : k + 1, :], 1.0, 0.0).astype(jnp.bfloat16)
        return carry

    lax.fori_loop(0, n_table // LANE, build_put, 0)

    group_rows = NX * rows
    for h in range(HALVES):
        drain(precv.at[h, pl.ds(slots, slot_total - slots)], y_r.at[h])
        for q in range(PARTS):
            block = jnp.dot(put[q * group_rows : (q + 1) * group_rows, :], precv[h], preferred_element_type=jnp.float32)
            for j in x_order:
                col[h, q, j] = block[j * rows : (j + 1) * rows].astype(jnp.bfloat16)
                x_copy(h, q, j).start()
            xacc[h, q] = block[0:rows]

    for h in range(HALVES):
        for q in range(PARTS):
            drain(xrecv.at[h, q, pl.ds(1, NX - 1)], x_r.at[h, q])
            total = xacc[h, q]
            for j in range(1, NX):
                total = total + xrecv[h, q, j].astype(jnp.float32)
            xacc[h, q] = total
            for i in range(z_part):
                zsend[h, q * z_part + i] = total[i * owned : (i + 1) * owned].astype(jnp.bfloat16)
            for k in z_order:
                if pos(k) // z_part == q:
                    z_copy(h, k).start()

    def build_take(k, carry):
        column = jnp.broadcast_to(even[pl.ds(k, 1), :], (LANE, LANE)).T
        for v in range(n_table // LANE):
            row = lax.broadcasted_iota(jnp.int32, (LANE, LANE), 1) + v * LANE
            take[pl.ds(pl.multiple_of(k * LANE, LANE), LANE), v * LANE : (v + 1) * LANE] = jnp.where(
                column == row, 1.0, 0.0).astype(jnp.bfloat16)
        return carry

    lax.fori_loop(0, n_y, build_take, 0)
    for copy in fetch[5:]:
        copy.wait()
    drain(idrecv.at[pl.ds(1, n_mem - 1)], id_s)
    for h in range(HALVES):
        drain(precv.at[h, pl.ds(slots, slot_total - slots)], y_s.at[h])
        drain(xrecv.at[h, :, pl.ds(1, NX - 1)], x_s.at[h])

    own_q, own_at = z_rows(0)
    sums = []
    for h in range(HALVES):
        drain(zrecv.at[h, pl.ds(1, n_z - 1)], z_r.at[h])
        total = xacc[h, own_q, own_at, :]
        for k in range(1, n_z):
            total = total + zrecv[h, k].astype(jnp.float32)
        sums.append(total)

    scale = lax.rsqrt(mdeg[...].astype(jnp.float32))
    diagonal = lax.broadcasted_iota(jnp.int32, (owned, owned), 0) == lax.broadcasted_iota(
        jnp.int32, (owned, owned), 1)
    scale = jnp.sum(jnp.where(diagonal, jnp.broadcast_to(scale, (owned, owned)), 0.0), axis=1, keepdims=True)
    neigh = jnp.concatenate(sums, axis=1) * scale
    embed = mrow[...].astype(jnp.float32)
    first = (embed + neigh).astype(jnp.bfloat16)
    second = (neigh * embed).astype(jnp.bfloat16)
    result = jnp.dot(first, w1[...], preferred_element_type=jnp.float32) + jnp.dot(
        second, w2[...], preferred_element_type=jnp.float32)
    new = jnp.where(result > 0, result, 0.2 * result).astype(jnp.bfloat16)
    for h in range(HALVES):
        table[h, own_q, 0, own_at, :] = new[:, h * LANE : (h + 1) * LANE]

    for h in range(HALVES):
        for k in reversed(z_order):
            gz_copy(h, k).start()
    newv[...] = new
    keep = [pltpu.make_async_copy(newv, newm, out_s.at[0])]
    keep[0].start()
    for h, q in ((0, 2), (0, 1), (1, 2), (0, 0), (1, 1), (1, 0)):
        n_here = z_part - (1 if q == own_q else 0)
        drain(table.at[h, q, 0, pl.ds(0, n_here * owned)], gz_r.at[h, q])
        for j in x_order:
            gx_copy(h, q, j).start()

    for h in range(HALVES):
        drain(table.at[h, :, pl.ds(1, NX - 1)], gx_r.at[h])
        for first in (4, 2, 6, 0):
            at = slice(first * LANE, (first + 2) * LANE)
            served[h, at, :] = jnp.dot(
                take[at, :], table[h].reshape(n_table, LANE), preferred_element_type=jnp.float32
            ).astype(jnp.bfloat16)
            for d in mem_order:
                if d[0] // 2 * 2 == first:
                    b_copy(h, *d).start()
        keep.append(pltpu.make_async_copy(served.at[h, pl.ds(0, slots)], mirror.at[mine, pl.ds(h * LANE, LANE)], out_s.at[1 + h]))
        keep[-1].start()

    for copy in keep:
        copy.wait()

    drain(zrecv.at[:, pl.ds(1, n_z - 1)], gz_s)
    for h in range(HALVES):
        drain(zrecv.at[h, pl.ds(1, n_z - 1)], z_s.at[h])
        drain(table.at[h, :, pl.ds(1, NX - 1)], gx_s.at[h])
    for h in range(HALVES):
        drain(served.at[h, pl.ds(slots, slot_total - slots)], b_s.at[h])
        drain(served.at[h, pl.ds(slots, slot_total - slots)], b_r.at[h])


def hand_over(new_in, mirror_in, new_out, mirror_out, new_v, mirror_v, in_s, out_s):
    piece = mirror_v.shape[0] // (in_s.shape[0] - 1)
    views = [(new_in, new_v, new_out)] + [
        (mirror_in.at[at], mirror_v.at[at], mirror_out.at[at])
        for at in (pl.ds(i * piece, piece) for i in range(in_s.shape[0] - 1))]
    inward = [pltpu.make_async_copy(a, b, in_s.at[i]) for i, (a, b, _) in enumerate(views)]
    outward = [pltpu.make_async_copy(b, c, out_s.at[i]) for i, (_, b, c) in enumerate(views)]
    for copy in inward:
        copy.start()
    for first, then in zip(inward, outward):
        first.wait()
        then.start()
    for copy in outward:
        copy.wait()


def body(n_grp, n_mem, source_rows, source_degree, edge_tiles, tile_row, tile_col, mirror_ids,
         master_rows, master_degree, weight_one, weight_two):
    n_tiles, tile, _ = edge_tiles.shape
    src_dev, width = source_rows.shape
    slot_total = mirror_ids.shape[0]
    owned = master_rows.shape[0]
    n_z = n_grp // NX
    z_part = n_z // PARTS
    rows = z_part * owned
    n_table = n_z * NX * owned
    hbm = pl.BlockSpec(memory_space=pltpu.HBM)
    vmem = pl.BlockSpec(memory_space=pltpu.VMEM)
    bf, f32, i32 = jnp.bfloat16, jnp.float32, jnp.int32
    dma = pltpu.SemaphoreType.DMA
    operands = (
        tile_row, tile_col, source_rows, source_degree.reshape(-1, tile), edge_tiles, mirror_ids.reshape(-1, LANE),
        master_rows, master_degree.reshape(1, owned), weight_one, weight_two,
    )
    outs = pl.pallas_call(
        functools.partial(kernel, n_grp, n_mem),
        out_shape=(
            jax.ShapeDtypeStruct((owned, width), bf),
            jax.ShapeDtypeStruct((slot_total, width), bf),
        ),
        in_specs=[hbm] * len(operands),
        out_specs=(hbm, hbm),
        scratch_shapes=[
            pltpu.SMEM((n_tiles,), i32),
            pltpu.SMEM((n_tiles,), i32),
            pltpu.VMEM((src_dev, width), bf),
            pltpu.VMEM((src_dev // tile, tile), i32),
            pltpu.VMEM((n_tiles, tile, tile), i32),
            pltpu.VMEM((slot_total // LANE, LANE), i32),
            pltpu.VMEM((owned, width), bf),
            pltpu.VMEM((1, owned), i32),
            pltpu.VMEM((width, width), bf),
            pltpu.VMEM((width, width), bf),
            pltpu.VMEM((HALVES, src_dev // tile, tile, LANE), bf),
            pltpu.VMEM((n_tiles, tile, tile), bf),
            pltpu.VMEM((n_mem // NC, tile, n_tiles * tile), bf),
            pltpu.VMEM((HALVES, n_tiles * tile, LANE), bf),
            pltpu.VMEM((HALVES, n_mem // NC, tile, LANE), bf),
            pltpu.VMEM((n_mem // NC, 1, LANE), i32),
            pltpu.VMEM((n_mem, 1, LANE), i32),
            pltpu.VMEM((slot_total // LANE, LANE), i32),
            pltpu.VMEM((slot_total // LANE, LANE), i32),
            pltpu.VMEM((n_table, slot_total), bf),
            pltpu.VMEM((slot_total, n_table), bf),
            pltpu.VMEM((HALVES, slot_total, LANE), bf),
            pltpu.VMEM((HALVES, PARTS, NX, rows, LANE), bf),
            pltpu.VMEM((HALVES, PARTS, rows, LANE), f32),
            pltpu.VMEM((HALVES, PARTS, NX, rows, LANE), bf),
            pltpu.VMEM((HALVES, n_z, owned, LANE), bf),
            pltpu.VMEM((HALVES, n_z, owned, LANE), bf),
            pltpu.VMEM((HALVES, PARTS, NX, rows, LANE), bf),
            pltpu.VMEM((HALVES, slot_total, LANE), bf),
            pltpu.VMEM((owned, width), bf), dma((1 + HALVES,)),
            dma((len(operands) - 1,)), dma((FETCH,)),
            dma, dma,
            dma((HALVES,)), dma((HALVES,)),
            dma((HALVES,)), dma((HALVES, PARTS)),
            dma((HALVES,)), dma((HALVES,)),
            dma, dma((HALVES, PARTS)),
            dma((HALVES,)), dma((HALVES,)),
            dma((HALVES,)), dma((HALVES,)),
        ],
        compiler_params=pltpu.CompilerParams(
            collective_id=0, has_side_effects=True, vmem_limit_bytes=62 * 2**20),
        name="layer",
    )(*operands)
    return pl.pallas_call(
        hand_over,
        out_shape=tuple(jax.ShapeDtypeStruct(o.shape, o.dtype) for o in outs),
        in_specs=[hbm, hbm],
        out_specs=(hbm, hbm),
        scratch_shapes=[pltpu.VMEM(o.shape, o.dtype) for o in outs] + [dma((5,)), dma((5,))],
        compiler_params=pltpu.CompilerParams(vmem_limit_bytes=62 * 2**20),
        name="hand_over",
    )(*outs)


def solution(mesh):
    both = ("grp", "mem")
    in_specs = (
        P(both, None), P(both), P(both, None, None), P(both), P(both), P(both),
        P(both, None), P(both), P(), P(),
    )
    out_specs = (P(both, None), P(both, None))
    fn = functools.partial(body, mesh.shape["grp"], mesh.shape["mem"])
    return jax.shard_map(fn, mesh=mesh, in_specs=in_specs, out_specs=out_specs, check_vma=False)
```

```python
import functools

import jax
import jax.numpy as jnp
from jax import lax
from jax.experimental import pallas as pl
from jax.experimental.pallas import tpu as pltpu
from jax.sharding import PartitionSpec as P

MESH = pl.DeviceIdType.MESH
NX = 4
NC = 2
LANE = 128
HALVES = 2
PARTS = 6
FETCH = 4


def log2(n):
    assert n & (n - 1) == 0
    return n.bit_length() - 1


def kernel(
    n_grp, n_mem, trow_h, tcol_h, src_h, deg_h, tiles_h, ids_h, mrow_h, mdeg_h, w1_h, w2_h, newm, mirror,
    trow, tcol, src, deg, tiles, idin, mrow, mdeg, w1, w2,
    scaled, bits, lhs, rhs, part, place, idrecv, even, odd, put, take, precv, col, xacc, xrecv, zsend, zrecv, table, served,
    newv, out_s, in_s, tile_s, id_s, id_r, y_s, y_r, x_s, x_r, z_s, z_r, gz_s, gz_r, gx_s, gx_r, b_s, b_r,
):
    g = lax.axis_index("grp")
    m = lax.axis_index("mem")
    n_z, n_y = n_grp // NX, n_mem // NC
    x, z = lax.rem(g, NX), g // NX
    c, y = lax.rem(m, NC), m // NC
    tile = tiles.shape[1]
    n_tiles = tiles.shape[0]
    slot_total = precv.shape[1]
    slots = slot_total // n_mem
    owned = mrow.shape[0]
    half_z = n_z // 2
    z_part = n_z // PARTS
    rows = z_part * owned

    def mem_of(dy, dc):
        return lax.rem(y + dy + n_y, n_y) * NC + lax.rem(c + dc, NC)

    def grp_x(j):
        return z * NX + lax.rem(x + j + NX, NX)

    def grp_z(k):
        return lax.rem(z + k + n_z, n_z) * NX + x

    def pos(k):
        return 2 * abs(k - half_z) - (1 if k < half_z else 0)

    y_order = [0] + [s for d in range(1, n_y // 2) for s in (n_y - d, d)] + [n_y // 2]
    mem_order = [(dy, dc) for dy in reversed(y_order) for dc in range(NC) if (dy, dc) != (0, 0)]
    x_order = sorted(range(1, NX), key=lambda j: -min(j, NX - j))
    z_order = sorted(range(1, n_z), key=pos)

    fetch = [
        pltpu.make_async_copy(a, b, in_s.at[i])
        for i, (a, b) in enumerate([
            (deg_h, deg), (src_h, src), (trow_h, trow), (tcol_h, tcol), (ids_h, idin),
            (mrow_h, mrow), (mdeg_h, mdeg), (w1_h, w1), (w2_h, w2)])
    ]
    step = n_tiles // FETCH
    fetch_tiles = [
        pltpu.make_async_copy(tiles_h.at[pl.ds(i * step, step)], tiles.at[pl.ds(i * step, step)], tile_s.at[i])
        for i in range(FETCH)
    ]
    for copy in fetch[:5]:
        copy.start()
    for copy in fetch_tiles:
        copy.start()
    for copy in fetch[5:]:
        copy.start()

    barrier = pltpu.get_barrier_semaphore()
    partners = [(grp_z(k), m) for k in z_order] + [(g, mem_of(*d)) for d in mem_order] + [
        (grp_x(j), m) for j in x_order]
    for who in partners:
        pl.semaphore_signal(barrier, inc=1, device_id=who, device_id_type=MESH)

    fetch[0].wait()
    fetch[1].wait()
    scale = lax.rsqrt(deg[...].astype(jnp.float32))
    for k in range(src.shape[0] // tile):
        column = jnp.broadcast_to(scale[k : k + 1, :], (tile, tile)).T
        for h in range(HALVES):
            at = (pl.ds(k * tile, tile), pl.ds(h * LANE, LANE))
            scaled[h, k] = (src[at].astype(jnp.float32) * column).astype(jnp.bfloat16)
    for copy in fetch[2:5]:
        copy.wait()

    ids = idin[...]
    group = jnp.right_shift(ids, log2(owned * n_mem))
    dx = jnp.bitwise_and(group, NX - 1) - x
    dx = jnp.where(dx < 0, dx + NX, dx)
    dz = jnp.right_shift(group, log2(NX)) - z
    dz = jnp.where(dz < 0, dz + n_z, dz)
    order = 2 * jnp.abs(dz - half_z) - jnp.where(dz < half_z, 1, 0)
    z_group = jnp.right_shift(order, log2(z_part))
    spots = (z_group * NX + dx) * rows + jnp.bitwise_and(order, z_part - 1) * owned + jnp.bitwise_and(
        ids, owned - 1)

    for k in range(n_y):
        place[k] = spots[k : k + 1, :]

    for i in range(FETCH):
        fetch_tiles[i].wait()
        for t in range(i * step, (i + 1) * step):
            bits[t] = tiles[t].astype(jnp.float32).astype(jnp.bfloat16)

    def sums_for(h, dy):
        block = lax.rem(y + dy, n_y)
        if h == 0:
            for t in range(n_tiles):
                edges = bits[t]
                lhs[dy, :, t * tile : (t + 1) * tile] = jnp.where(trow[t] == block, edges, jnp.zeros_like(edges))
        part[h, dy] = jnp.dot(lhs[dy], rhs[h], preferred_element_type=jnp.float32).astype(jnp.bfloat16)


    def slot_of(dy, dc):
        return dy * NC + dc

    def id_copy(dy, dc):
        return pltpu.make_async_remote_copy(
            src_ref=place.at[lax.rem(y + dy, n_y)], dst_ref=idrecv.at[slot_of(dy, dc)], send_sem=id_s, recv_sem=id_r,
            device_id=(g, mem_of(dy, dc)), device_id_type=MESH)

    def y_copy(h, dy, dc):
        to = mem_of(dy, dc)
        return pltpu.make_async_remote_copy(
            src_ref=part.at[h, dy, pl.ds(pl.multiple_of(lax.rem(to, NC) * slots, slots), slots)],
            dst_ref=precv.at[h, pl.ds(slot_of(dy, dc) * slots, slots)],
            send_sem=y_s.at[h], recv_sem=y_r.at[h], device_id=(g, to), device_id_type=MESH)

    def x_copy(h, q, j):
        return pltpu.make_async_remote_copy(
            src_ref=col.at[h, q, j], dst_ref=xrecv.at[h, q, j], send_sem=x_s.at[h], recv_sem=x_r.at[h, q],
            device_id=(grp_x(j), m), device_id_type=MESH)

    def z_copy(h, k):
        return pltpu.make_async_remote_copy(
            src_ref=zsend.at[h, pos(k)], dst_ref=zrecv.at[h, k], send_sem=z_s.at[h], recv_sem=z_r.at[h],
            device_id=(grp_z(k), m), device_id_type=MESH)

    def z_rows(k):
        return pos(k) // z_part, pl.ds(pos(k) % z_part * owned, owned)

    def gz_copy(h, k):
        q, at = z_rows(0)
        to_q, to_at = z_rows((n_z - k) % n_z)
        return pltpu.make_async_remote_copy(
            src_ref=table.at[h, q, 0, at], dst_ref=table.at[h, to_q, 0, to_at], send_sem=gz_s,
            recv_sem=gz_r.at[h, to_q], device_id=(grp_z(k), m), device_id_type=MESH)

    def gx_copy(h, q, j):
        return pltpu.make_async_remote_copy(
            src_ref=table.at[h, q, 0], dst_ref=table.at[h, q, NX - j], send_sem=gx_s.at[h], recv_sem=gx_r.at[h],
            device_id=(grp_x(j), m), device_id_type=MESH)

    def b_copy(h, dy, dc):
        to = mem_of(-dy, dc)
        return pltpu.make_async_remote_copy(
            src_ref=served.at[h, pl.ds(slot_of(dy, dc) * slots, slots)],
            dst_ref=mirror.at[pl.ds(pl.multiple_of(m * slots, slots), slots), pl.ds(h * LANE, LANE)],
            send_sem=b_s.at[h], recv_sem=b_r.at[h], device_id=(g, to), device_id_type=MESH)

    def drain(ref, sem):
        pltpu.make_async_copy(ref, ref, sem).wait()

    mine = pl.ds(pl.multiple_of(m * slots, slots), slots)
    idrecv[0] = place[y]
    for h in range(HALVES):
        for t in range(n_tiles):
            rhs[h, t * tile : (t + 1) * tile, :] = scaled[h, tcol[t]]
        for i, dy in enumerate(reversed(y_order)):
            sums_for(h, dy)
            if h == 0 and i == 0:
                pl.semaphore_wait(barrier, len(partners))
                for d in mem_order:
                    id_copy(*d).start()
            for dc in range(NC):
                if (dy, dc) != (0, 0):
                    y_copy(h, dy, dc).start()
        precv[h, 0:slots] = part[h, 0, pl.ds(pl.multiple_of(c * slots, slots), slots), :]

    drain(idrecv.at[pl.ds(1, n_mem - 1)], id_r)
    for k in range(n_y):
        even[k : k + 1, :] = idrecv[NC * k]
        odd[k : k + 1, :] = idrecv[NC * k + 1]
    lane = lax.broadcasted_iota(jnp.int32, (n_y, LANE), 1)
    low = jnp.where(c == 0, even[...], pltpu.roll(even[...], slots, 1))
    high = jnp.where(c == 0, pltpu.roll(odd[...], slots, 1), odd[...])
    spot = jnp.where(lane < slots, low, high)
    n_table = PARTS * NX * rows
    even[...] = spot

    def build_put(v, carry):
        row = lax.broadcasted_iota(jnp.int32, (LANE, LANE), 0) + v * LANE
        for k in range(n_y):
            put[pl.ds(pl.multiple_of(v * LANE, LANE), LANE), k * LANE : (k + 1) * LANE] = jnp.where(
                row == even[k : k + 1, :], 1.0, 0.0).astype(jnp.bfloat16)
        return carry

    lax.fori_loop(0, n_table // LANE, build_put, 0)

    group_rows = NX * rows
    for h in range(HALVES):
        drain(precv.at[h, pl.ds(slots, slot_total - slots)], y_r.at[h])
        for q in range(PARTS):
            block = jnp.dot(put[q * group_rows : (q + 1) * group_rows, :], precv[h], preferred_element_type=jnp.float32)
            for j in x_order:
                col[h, q, j] = block[j * rows : (j + 1) * rows].astype(jnp.bfloat16)
                x_copy(h, q, j).start()
            xacc[h, q] = block[0:rows]

    for h in range(HALVES):
        for q in range(PARTS):
            drain(xrecv.at[h, q, pl.ds(1, NX - 1)], x_r.at[h, q])
            total = xacc[h, q]
            for j in range(1, NX):
                total = total + xrecv[h, q, j].astype(jnp.float32)
            xacc[h, q] = total
            for i in range(z_part):
                zsend[h, q * z_part + i] = total[i * owned : (i + 1) * owned].astype(jnp.bfloat16)
            for k in z_order:
                if pos(k) // z_part == q:
                    z_copy(h, k).start()

    def build_take(k, carry):
        column = jnp.broadcast_to(even[pl.ds(k, 1), :], (LANE, LANE)).T
        for v in range(n_table // LANE):
            row = lax.broadcasted_iota(jnp.int32, (LANE, LANE), 1) + v * LANE
            take[pl.ds(pl.multiple_of(k * LANE, LANE), LANE), v * LANE : (v + 1) * LANE] = jnp.where(
                column == row, 1.0, 0.0).astype(jnp.bfloat16)
        return carry

    lax.fori_loop(0, n_y, build_take, 0)
    for copy in fetch[5:]:
        copy.wait()
    drain(idrecv.at[pl.ds(1, n_mem - 1)], id_s)
    for h in range(HALVES):
        drain(precv.at[h, pl.ds(slots, slot_total - slots)], y_s.at[h])
        drain(xrecv.at[h, :, pl.ds(1, NX - 1)], x_s.at[h])

    own_q, own_at = z_rows(0)
    sums = []
    for h in range(HALVES):
        drain(zrecv.at[h, pl.ds(1, n_z - 1)], z_r.at[h])
        total = xacc[h, own_q, own_at, :]
        for k in range(1, n_z):
            total = total + zrecv[h, k].astype(jnp.float32)
        sums.append(total)

    scale = lax.rsqrt(mdeg[...].astype(jnp.float32))
    diagonal = lax.broadcasted_iota(jnp.int32, (owned, owned), 0) == lax.broadcasted_iota(
        jnp.int32, (owned, owned), 1)
    scale = jnp.sum(jnp.where(diagonal, jnp.broadcast_to(scale, (owned, owned)), 0.0), axis=1, keepdims=True)
    neigh = jnp.concatenate(sums, axis=1) * scale
    embed = mrow[...].astype(jnp.float32)
    first = (embed + neigh).astype(jnp.bfloat16)
    second = (neigh * embed).astype(jnp.bfloat16)
    result = jnp.dot(first, w1[...], preferred_element_type=jnp.float32) + jnp.dot(
        second, w2[...], preferred_element_type=jnp.float32)
    new = jnp.where(result > 0, result, 0.2 * result).astype(jnp.bfloat16)
    for h in range(HALVES):
        table[h, own_q, 0, own_at, :] = new[:, h * LANE : (h + 1) * LANE]

    for k in reversed(z_order):
        gz_copy(0, k).start()
    newv[...] = new
    keep = [pltpu.make_async_copy(newv, newm, out_s.at[0])]
    keep[0].start()
    for h in range(HALVES):
        for q in reversed(range(PARTS)):
            n_here = z_part - (1 if q == own_q else 0)
            drain(table.at[h, q, 0, pl.ds(0, n_here * owned)], gz_r.at[h, q])
            for j in x_order:
                gx_copy(h, q, j).start()
            if (h, q) == (0, PARTS // 2):
                for k in reversed(z_order):
                    gz_copy(1, k).start()

    for h in range(HALVES):
        drain(table.at[h, :, pl.ds(1, NX - 1)], gx_r.at[h])
        for first in (4, 2, 6, 0):
            at = slice(first * LANE, (first + 2) * LANE)
            served[h, at, :] = jnp.dot(
                take[at, :], table[h].reshape(n_table, LANE), preferred_element_type=jnp.float32
            ).astype(jnp.bfloat16)
            for d in mem_order:
                if d[0] // 2 * 2 == first:
                    b_copy(h, *d).start()
        keep.append(pltpu.make_async_copy(served.at[h, pl.ds(0, slots)], mirror.at[mine, pl.ds(h * LANE, LANE)], out_s.at[1 + h]))
        keep[-1].start()

    for copy in keep:
        copy.wait()

    drain(zrecv.at[:, pl.ds(1, n_z - 1)], gz_s)
    for h in range(HALVES):
        drain(zrecv.at[h, pl.ds(1, n_z - 1)], z_s.at[h])
        drain(table.at[h, :, pl.ds(1, NX - 1)], gx_s.at[h])
    for h in range(HALVES):
        drain(served.at[h, pl.ds(slots, slot_total - slots)], b_s.at[h])
        drain(served.at[h, pl.ds(slots, slot_total - slots)], b_r.at[h])


def hand_over(new_in, mirror_in, new_out, mirror_out, new_v, mirror_v, in_s, out_s):
    piece = mirror_v.shape[0] // (in_s.shape[0] - 1)
    views = [(new_in, new_v, new_out)] + [
        (mirror_in.at[at], mirror_v.at[at], mirror_out.at[at])
        for at in (pl.ds(i * piece, piece) for i in range(in_s.shape[0] - 1))]
    inward = [pltpu.make_async_copy(a, b, in_s.at[i]) for i, (a, b, _) in enumerate(views)]
    outward = [pltpu.make_async_copy(b, c, out_s.at[i]) for i, (_, b, c) in enumerate(views)]
    for copy in inward:
        copy.start()
    for first, then in zip(inward, outward):
        first.wait()
        then.start()
    for copy in outward:
        copy.wait()


def body(n_grp, n_mem, source_rows, source_degree, edge_tiles, tile_row, tile_col, mirror_ids,
         master_rows, master_degree, weight_one, weight_two):
    n_tiles, tile, _ = edge_tiles.shape
    src_dev, width = source_rows.shape
    slot_total = mirror_ids.shape[0]
    owned = master_rows.shape[0]
    n_z = n_grp // NX
    z_part = n_z // PARTS
    rows = z_part * owned
    n_table = n_z * NX * owned
    hbm = pl.BlockSpec(memory_space=pltpu.HBM)
    vmem = pl.BlockSpec(memory_space=pltpu.VMEM)
    bf, f32, i32 = jnp.bfloat16, jnp.float32, jnp.int32
    dma = pltpu.SemaphoreType.DMA
    operands = (
        tile_row, tile_col, source_rows, source_degree.reshape(-1, tile), edge_tiles, mirror_ids.reshape(-1, LANE),
        master_rows, master_degree.reshape(1, owned), weight_one, weight_two,
    )
    outs = pl.pallas_call(
        functools.partial(kernel, n_grp, n_mem),
        out_shape=(
            jax.ShapeDtypeStruct((owned, width), bf),
            jax.ShapeDtypeStruct((slot_total, width), bf),
        ),
        in_specs=[hbm] * len(operands),
        out_specs=(hbm, hbm),
        scratch_shapes=[
            pltpu.SMEM((n_tiles,), i32),
            pltpu.SMEM((n_tiles,), i32),
            pltpu.VMEM((src_dev, width), bf),
            pltpu.VMEM((src_dev // tile, tile), i32),
            pltpu.VMEM((n_tiles, tile, tile), i32),
            pltpu.VMEM((slot_total // LANE, LANE), i32),
            pltpu.VMEM((owned, width), bf),
            pltpu.VMEM((1, owned), i32),
            pltpu.VMEM((width, width), bf),
            pltpu.VMEM((width, width), bf),
            pltpu.VMEM((HALVES, src_dev // tile, tile, LANE), bf),
            pltpu.VMEM((n_tiles, tile, tile), bf),
            pltpu.VMEM((n_mem // NC, tile, n_tiles * tile), bf),
            pltpu.VMEM((HALVES, n_tiles * tile, LANE), bf),
            pltpu.VMEM((HALVES, n_mem // NC, tile, LANE), bf),
            pltpu.VMEM((n_mem // NC, 1, LANE), i32),
            pltpu.VMEM((n_mem, 1, LANE), i32),
            pltpu.VMEM((slot_total // LANE, LANE), i32),
            pltpu.VMEM((slot_total // LANE, LANE), i32),
            pltpu.VMEM((n_table, slot_total), bf),
            pltpu.VMEM((slot_total, n_table), bf),
            pltpu.VMEM((HALVES, slot_total, LANE), bf),
            pltpu.VMEM((HALVES, PARTS, NX, rows, LANE), bf),
            pltpu.VMEM((HALVES, PARTS, rows, LANE), f32),
            pltpu.VMEM((HALVES, PARTS, NX, rows, LANE), bf),
            pltpu.VMEM((HALVES, n_z, owned, LANE), bf),
            pltpu.VMEM((HALVES, n_z, owned, LANE), bf),
            pltpu.VMEM((HALVES, PARTS, NX, rows, LANE), bf),
            pltpu.VMEM((HALVES, slot_total, LANE), bf),
            pltpu.VMEM((owned, width), bf), dma((1 + HALVES,)),
            dma((len(operands) - 1,)), dma((FETCH,)),
            dma, dma,
            dma((HALVES,)), dma((HALVES,)),
            dma((HALVES,)), dma((HALVES, PARTS)),
            dma((HALVES,)), dma((HALVES,)),
            dma, dma((HALVES, PARTS)),
            dma((HALVES,)), dma((HALVES,)),
            dma((HALVES,)), dma((HALVES,)),
        ],
        compiler_params=pltpu.CompilerParams(
            collective_id=0, has_side_effects=True, vmem_limit_bytes=62 * 2**20),
        name="layer",
    )(*operands)
    return pl.pallas_call(
        hand_over,
        out_shape=tuple(jax.ShapeDtypeStruct(o.shape, o.dtype) for o in outs),
        in_specs=[hbm, hbm],
        out_specs=(hbm, hbm),
        scratch_shapes=[pltpu.VMEM(o.shape, o.dtype) for o in outs] + [dma((5,)), dma((5,))],
        compiler_params=pltpu.CompilerParams(vmem_limit_bytes=62 * 2**20),
        name="hand_over",
    )(*outs)


def solution(mesh):
    both = ("grp", "mem")
    in_specs = (
        P(both, None), P(both), P(both, None, None), P(both), P(both), P(both),
        P(both, None), P(both), P(), P(),
    )
    out_specs = (P(both, None), P(both, None))
    fn = functools.partial(body, mesh.shape["grp"], mesh.shape["mem"])
    return jax.shard_map(fn, mesh=mesh, in_specs=in_specs, out_specs=out_specs, check_vma=False)
```

```python
import functools

import jax
import jax.numpy as jnp
from jax import lax
from jax.experimental import pallas as pl
from jax.experimental.pallas import tpu as pltpu
from jax.sharding import PartitionSpec as P

MESH = pl.DeviceIdType.MESH
NX = 4
NC = 2
LANE = 128
HALVES = 2
PARTS = 6
FETCH = 4


def log2(n):
    assert n & (n - 1) == 0
    return n.bit_length() - 1


def kernel(
    n_grp, n_mem, trow_h, tcol_h, src_h, deg_h, tiles_h, ids_h, mrow_h, mdeg_h, w1_h, w2_h, newm, mirror,
    trow, tcol, src, deg, tiles, idin, mrow, mdeg, w1, w2,
    scaled, bits, lhs, rhs, part, place, idrecv, even, odd, put, take, precv, col, xacc, xrecv, zsend, zrecv, table, served,
    newv, out_s, up_s, down_s, in_s, tile_s, id_s, id_r, y_s, y_r, x_s, x_r, z_s, z_r, gz_s, gz_r, gx_s, gx_r, b_s, b_r,
):
    g = lax.axis_index("grp")
    m = lax.axis_index("mem")
    n_z, n_y = n_grp // NX, n_mem // NC
    x, z = lax.rem(g, NX), g // NX
    c, y = lax.rem(m, NC), m // NC
    tile = tiles.shape[1]
    n_tiles = tiles.shape[0]
    slot_total = precv.shape[1]
    slots = slot_total // n_mem
    owned = mrow.shape[0]
    half_z = n_z // 2
    z_part = n_z // PARTS
    rows = z_part * owned

    def mem_of(dy, dc):
        return lax.rem(y + dy + n_y, n_y) * NC + lax.rem(c + dc, NC)

    def grp_x(j):
        return z * NX + lax.rem(x + j + NX, NX)

    def grp_z(k):
        return lax.rem(z + k + n_z, n_z) * NX + x

    def pos(k):
        return 2 * abs(k - half_z) - (1 if k < half_z else 0)

    y_order = [0] + [s for d in range(1, n_y // 2) for s in (n_y - d, d)] + [n_y // 2]
    mem_order = [(dy, dc) for dy in reversed(y_order) for dc in range(NC) if (dy, dc) != (0, 0)]
    x_order = sorted(range(1, NX), key=lambda j: -min(j, NX - j))
    z_order = sorted(range(1, n_z), key=pos)

    fetch = [
        pltpu.make_async_copy(a, b, in_s.at[i])
        for i, (a, b) in enumerate([
            (deg_h, deg), (src_h, src), (trow_h, trow), (tcol_h, tcol), (ids_h, idin),
            (mrow_h, mrow), (mdeg_h, mdeg), (w1_h, w1), (w2_h, w2)])
    ]
    step = n_tiles // FETCH
    fetch_tiles = [
        pltpu.make_async_copy(tiles_h.at[pl.ds(i * step, step)], tiles.at[pl.ds(i * step, step)], tile_s.at[i])
        for i in range(FETCH)
    ]
    for copy in fetch[:5]:
        copy.start()
    for copy in fetch_tiles:
        copy.start()
    for copy in fetch[5:]:
        copy.start()

    barrier = pltpu.get_barrier_semaphore()
    partners = [(g, mem_of(*d)) for d in mem_order] + [(grp_x(j), m) for j in x_order] + [
        (grp_z(k), m) for k in (1, n_z - 1)]
    for who in partners:
        pl.semaphore_signal(barrier, inc=1, device_id=who, device_id_type=MESH)

    fetch[0].wait()
    fetch[1].wait()
    scale = lax.rsqrt(deg[...].astype(jnp.float32))
    for k in range(src.shape[0] // tile):
        column = jnp.broadcast_to(scale[k : k + 1, :], (tile, tile)).T
        for h in range(HALVES):
            at = (pl.ds(k * tile, tile), pl.ds(h * LANE, LANE))
            scaled[h, k] = (src[at].astype(jnp.float32) * column).astype(jnp.bfloat16)
    for copy in fetch[2:5]:
        copy.wait()

    ids = idin[...]
    group = jnp.right_shift(ids, log2(owned * n_mem))
    dx = jnp.bitwise_and(group, NX - 1) - x
    dx = jnp.where(dx < 0, dx + NX, dx)
    dz = jnp.right_shift(group, log2(NX)) - z
    dz = jnp.where(dz < 0, dz + n_z, dz)
    order = 2 * jnp.abs(dz - half_z) - jnp.where(dz < half_z, 1, 0)
    z_group = jnp.right_shift(order, log2(z_part))
    spots = (z_group * NX + dx) * rows + jnp.bitwise_and(order, z_part - 1) * owned + jnp.bitwise_and(
        ids, owned - 1)

    for k in range(n_y):
        place[k] = spots[k : k + 1, :]

    def fill_rhs(h):
        for t in range(n_tiles):
            rhs[h, t * tile : (t + 1) * tile, :] = scaled[h, tcol[t]]

    fill_rhs(0)
    for i in range(FETCH):
        fetch_tiles[i].wait()
        for t in range(i * step, (i + 1) * step):
            bits[t] = tiles[t].astype(jnp.float32).astype(jnp.bfloat16)

    def sums_for(h, dy):
        block = lax.rem(y + dy, n_y)
        if h == 0:
            for t in range(n_tiles):
                edges = bits[t]
                lhs[dy, :, t * tile : (t + 1) * tile] = jnp.where(trow[t] == block, edges, jnp.zeros_like(edges))
        part[h, dy] = jnp.dot(lhs[dy], rhs[h], preferred_element_type=jnp.float32).astype(jnp.bfloat16)


    def slot_of(dy, dc):
        return dy * NC + dc

    def id_copy(dy, dc):
        return pltpu.make_async_remote_copy(
            src_ref=place.at[lax.rem(y + dy, n_y)], dst_ref=idrecv.at[slot_of(dy, dc)], send_sem=id_s, recv_sem=id_r,
            device_id=(g, mem_of(dy, dc)), device_id_type=MESH)

    def y_copy(h, dy, dc):
        to = mem_of(dy, dc)
        return pltpu.make_async_remote_copy(
            src_ref=part.at[h, dy, pl.ds(pl.multiple_of(lax.rem(to, NC) * slots, slots), slots)],
            dst_ref=precv.at[h, pl.ds(slot_of(dy, dc) * slots, slots)],
            send_sem=y_s.at[h], recv_sem=y_r.at[h], device_id=(g, to), device_id_type=MESH)

    def x_copy(h, q, j):
        return pltpu.make_async_remote_copy(
            src_ref=col.at[h, q, j], dst_ref=xrecv.at[h, q, j], send_sem=x_s.at[h], recv_sem=x_r.at[h, q],
            device_id=(grp_x(j), m), device_id_type=MESH)

    def z_copy(h, k):
        return pltpu.make_async_remote_copy(
            src_ref=zsend.at[h, pos(k)], dst_ref=zrecv.at[h, k], send_sem=z_s.at[h], recv_sem=z_r.at[h],
            device_id=(grp_z(k), m), device_id_type=MESH)

    def z_rows(k):
        return pos(k) // z_part, pl.ds(pos(k) % z_part * owned, owned)

    def gz_copy(h, k):
        q, at = z_rows(0)
        to_q, to_at = z_rows((n_z - k) % n_z)
        return pltpu.make_async_remote_copy(
            src_ref=table.at[h, q, 0, at], dst_ref=table.at[h, to_q, 0, to_at], send_sem=gz_s,
            recv_sem=gz_r.at[h, to_q], device_id=(grp_z(k), m), device_id_type=MESH)

    def gx_copy(h, q, j):
        return pltpu.make_async_remote_copy(
            src_ref=table.at[h, q, 0], dst_ref=table.at[h, q, NX - j], send_sem=gx_s.at[h], recv_sem=gx_r.at[h],
            device_id=(grp_x(j), m), device_id_type=MESH)

    def b_copy(h, dy, dc):
        to = mem_of(-dy, dc)
        return pltpu.make_async_remote_copy(
            src_ref=served.at[h, pl.ds(slot_of(dy, dc) * slots, slots)],
            dst_ref=mirror.at[pl.ds(pl.multiple_of(m * slots, slots), slots), pl.ds(h * LANE, LANE)],
            send_sem=b_s.at[h], recv_sem=b_r.at[h], device_id=(g, to), device_id_type=MESH)

    def tell(r):
        if r < half_z - 1:
            pl.semaphore_signal(up_s.at[r], inc=1, device_id=(grp_z(1), m), device_id_type=MESH)
            pl.semaphore_signal(down_s.at[r], inc=1, device_id=(grp_z(n_z - 1), m), device_id_type=MESH)

    def hear(r):
        pl.semaphore_wait(up_s.at[r], 1)
        pl.semaphore_wait(down_s.at[r], 1)
        tell(r + 1)

    def drain(ref, sem):
        pltpu.make_async_copy(ref, ref, sem).wait()

    mine = pl.ds(pl.multiple_of(m * slots, slots), slots)
    idrecv[0] = place[y]
    for h in range(HALVES):
        if h:
            fill_rhs(h)
        for i, dy in enumerate(reversed(y_order)):
            sums_for(h, dy)
            if h == 0 and i == 0:
                pl.semaphore_wait(barrier, len(partners))
            for dc in range(NC):
                if (dy, dc) != (0, 0):
                    y_copy(h, dy, dc).start()
            if h == 0 and i == 0:
                tell(0)
            if h == 0 and i == 2:
                for d in mem_order:
                    id_copy(*d).start()
        precv[h, 0:slots] = part[h, 0, pl.ds(pl.multiple_of(c * slots, slots), slots), :]

    hear(0)
    drain(idrecv.at[pl.ds(1, n_mem - 1)], id_r)
    for k in range(n_y):
        even[k : k + 1, :] = idrecv[NC * k]
        odd[k : k + 1, :] = idrecv[NC * k + 1]
    lane = lax.broadcasted_iota(jnp.int32, (n_y, LANE), 1)
    low = jnp.where(c == 0, even[...], pltpu.roll(even[...], slots, 1))
    high = jnp.where(c == 0, pltpu.roll(odd[...], slots, 1), odd[...])
    spot = jnp.where(lane < slots, low, high)
    n_table = PARTS * NX * rows
    even[...] = spot

    def build_put(v, carry):
        row = lax.broadcasted_iota(jnp.int32, (LANE, LANE), 0) + v * LANE
        for k in range(n_y):
            put[pl.ds(pl.multiple_of(v * LANE, LANE), LANE), k * LANE : (k + 1) * LANE] = jnp.where(
                row == even[k : k + 1, :], 1.0, 0.0).astype(jnp.bfloat16)
        return carry

    lax.fori_loop(0, n_table // LANE, build_put, 0)

    hear(1)

    group_rows = NX * rows
    for h in range(HALVES):
        drain(precv.at[h, pl.ds(slots, slot_total - slots)], y_r.at[h])
        for q in range(PARTS):
            block = jnp.dot(put[q * group_rows : (q + 1) * group_rows, :], precv[h], preferred_element_type=jnp.float32)
            for j in x_order:
                col[h, q, j] = block[j * rows : (j + 1) * rows].astype(jnp.bfloat16)
                x_copy(h, q, j).start()
            xacc[h, q] = block[0:rows]
        if h == 0:
            for r in range(2, half_z - 1):
                hear(r)

    for h in range(HALVES):
        for q in range(PARTS):
            drain(xrecv.at[h, q, pl.ds(1, NX - 1)], x_r.at[h, q])
            total = xacc[h, q]
            for j in range(1, NX):
                total = total + xrecv[h, q, j].astype(jnp.float32)
            xacc[h, q] = total
            for i in range(z_part):
                zsend[h, q * z_part + i] = total[i * owned : (i + 1) * owned].astype(jnp.bfloat16)
            for k in z_order:
                if pos(k) // z_part == q:
                    z_copy(h, k).start()

    def build_take(k, carry):
        column = jnp.broadcast_to(even[pl.ds(k, 1), :], (LANE, LANE)).T
        for v in range(n_table // LANE):
            row = lax.broadcasted_iota(jnp.int32, (LANE, LANE), 1) + v * LANE
            take[pl.ds(pl.multiple_of(k * LANE, LANE), LANE), v * LANE : (v + 1) * LANE] = jnp.where(
                column == row, 1.0, 0.0).astype(jnp.bfloat16)
        return carry

    lax.fori_loop(0, n_y, build_take, 0)
    for copy in fetch[5:]:
        copy.wait()
    drain(idrecv.at[pl.ds(1, n_mem - 1)], id_s)
    for h in range(HALVES):
        drain(precv.at[h, pl.ds(slots, slot_total - slots)], y_s.at[h])
        drain(xrecv.at[h, :, pl.ds(1, NX - 1)], x_s.at[h])

    own_q, own_at = z_rows(0)
    sums = []
    for h in range(HALVES):
        drain(zrecv.at[h, pl.ds(1, n_z - 1)], z_r.at[h])
        total = xacc[h, own_q, own_at, :]
        for k in range(1, n_z):
            total = total + zrecv[h, k].astype(jnp.float32)
        sums.append(total)

    scale = lax.rsqrt(mdeg[...].astype(jnp.float32))
    diagonal = lax.broadcasted_iota(jnp.int32, (owned, owned), 0) == lax.broadcasted_iota(
        jnp.int32, (owned, owned), 1)
    scale = jnp.sum(jnp.where(diagonal, jnp.broadcast_to(scale, (owned, owned)), 0.0), axis=1, keepdims=True)
    neigh = jnp.concatenate(sums, axis=1) * scale
    embed = mrow[...].astype(jnp.float32)
    first = (embed + neigh).astype(jnp.bfloat16)
    second = (neigh * embed).astype(jnp.bfloat16)
    result = jnp.dot(first, w1[...], preferred_element_type=jnp.float32) + jnp.dot(
        second, w2[...], preferred_element_type=jnp.float32)
    new = jnp.where(result > 0, result, 0.2 * result).astype(jnp.bfloat16)
    for h in range(HALVES):
        table[h, own_q, 0, own_at, :] = new[:, h * LANE : (h + 1) * LANE]

    for k in reversed(z_order):
        gz_copy(0, k).start()
    newv[...] = new
    keep = [pltpu.make_async_copy(newv, newm, out_s.at[0])]
    keep[0].start()
    for h in range(HALVES):
        for q in reversed(range(PARTS)):
            n_here = z_part - (1 if q == own_q else 0)
            drain(table.at[h, q, 0, pl.ds(0, n_here * owned)], gz_r.at[h, q])
            for j in x_order:
                gx_copy(h, q, j).start()
            if (h, q) == (0, PARTS // 2):
                for k in reversed(z_order):
                    gz_copy(1, k).start()

    for h in range(HALVES):
        drain(table.at[h, :, pl.ds(1, NX - 1)], gx_r.at[h])
        for first in (4, 2, 6, 0):
            at = slice(first * LANE, (first + 2) * LANE)
            served[h, at, :] = jnp.dot(
                take[at, :], table[h].reshape(n_table, LANE), preferred_element_type=jnp.float32
            ).astype(jnp.bfloat16)
            for d in mem_order:
                if d[0] // 2 * 2 == first:
                    b_copy(h, *d).start()
        keep.append(pltpu.make_async_copy(served.at[h, pl.ds(0, slots)], mirror.at[mine, pl.ds(h * LANE, LANE)], out_s.at[1 + h]))
        keep[-1].start()

    for copy in keep:
        copy.wait()

    drain(zrecv.at[:, pl.ds(1, n_z - 1)], gz_s)
    for h in range(HALVES):
        drain(zrecv.at[h, pl.ds(1, n_z - 1)], z_s.at[h])
        drain(table.at[h, :, pl.ds(1, NX - 1)], gx_s.at[h])
    for h in range(HALVES):
        drain(served.at[h, pl.ds(slots, slot_total - slots)], b_s.at[h])
        drain(served.at[h, pl.ds(slots, slot_total - slots)], b_r.at[h])


def hand_over(new_in, mirror_in, new_out, mirror_out, new_v, mirror_v, in_s, out_s):
    piece = mirror_v.shape[0] // (in_s.shape[0] - 1)
    views = [(new_in, new_v, new_out)] + [
        (mirror_in.at[at], mirror_v.at[at], mirror_out.at[at])
        for at in (pl.ds(i * piece, piece) for i in range(in_s.shape[0] - 1))]
    inward = [pltpu.make_async_copy(a, b, in_s.at[i]) for i, (a, b, _) in enumerate(views)]
    outward = [pltpu.make_async_copy(b, c, out_s.at[i]) for i, (_, b, c) in enumerate(views)]
    for copy in inward:
        copy.start()
    for first, then in zip(inward, outward):
        first.wait()
        then.start()
    for copy in outward:
        copy.wait()


def body(n_grp, n_mem, source_rows, source_degree, edge_tiles, tile_row, tile_col, mirror_ids,
         master_rows, master_degree, weight_one, weight_two):
    n_tiles, tile, _ = edge_tiles.shape
    src_dev, width = source_rows.shape
    slot_total = mirror_ids.shape[0]
    owned = master_rows.shape[0]
    n_z = n_grp // NX
    z_part = n_z // PARTS
    rows = z_part * owned
    n_table = n_z * NX * owned
    hbm = pl.BlockSpec(memory_space=pltpu.HBM)
    vmem = pl.BlockSpec(memory_space=pltpu.VMEM)
    bf, f32, i32 = jnp.bfloat16, jnp.float32, jnp.int32
    dma = pltpu.SemaphoreType.DMA
    operands = (
        tile_row, tile_col, source_rows, source_degree.reshape(-1, tile), edge_tiles, mirror_ids.reshape(-1, LANE),
        master_rows, master_degree.reshape(1, owned), weight_one, weight_two,
    )
    outs = pl.pallas_call(
        functools.partial(kernel, n_grp, n_mem),
        out_shape=(
            jax.ShapeDtypeStruct((owned, width), bf),
            jax.ShapeDtypeStruct((slot_total, width), bf),
        ),
        in_specs=[hbm] * len(operands),
        out_specs=(hbm, hbm),
        scratch_shapes=[
            pltpu.SMEM((n_tiles,), i32),
            pltpu.SMEM((n_tiles,), i32),
            pltpu.VMEM((src_dev, width), bf),
            pltpu.VMEM((src_dev // tile, tile), i32),
            pltpu.VMEM((n_tiles, tile, tile), i32),
            pltpu.VMEM((slot_total // LANE, LANE), i32),
            pltpu.VMEM((owned, width), bf),
            pltpu.VMEM((1, owned), i32),
            pltpu.VMEM((width, width), bf),
            pltpu.VMEM((width, width), bf),
            pltpu.VMEM((HALVES, src_dev // tile, tile, LANE), bf),
            pltpu.VMEM((n_tiles, tile, tile), bf),
            pltpu.VMEM((n_mem // NC, tile, n_tiles * tile), bf),
            pltpu.VMEM((HALVES, n_tiles * tile, LANE), bf),
            pltpu.VMEM((HALVES, n_mem // NC, tile, LANE), bf),
            pltpu.VMEM((n_mem // NC, 1, LANE), i32),
            pltpu.VMEM((n_mem, 1, LANE), i32),
            pltpu.VMEM((slot_total // LANE, LANE), i32),
            pltpu.VMEM((slot_total // LANE, LANE), i32),
            pltpu.VMEM((n_table, slot_total), bf),
            pltpu.VMEM((slot_total, n_table), bf),
            pltpu.VMEM((HALVES, slot_total, LANE), bf),
            pltpu.VMEM((HALVES, PARTS, NX, rows, LANE), bf),
            pltpu.VMEM((HALVES, PARTS, rows, LANE), f32),
            pltpu.VMEM((HALVES, PARTS, NX, rows, LANE), bf),
            pltpu.VMEM((HALVES, n_z, owned, LANE), bf),
            pltpu.VMEM((HALVES, n_z, owned, LANE), bf),
            pltpu.VMEM((HALVES, PARTS, NX, rows, LANE), bf),
            pltpu.VMEM((HALVES, slot_total, LANE), bf),
            pltpu.VMEM((owned, width), bf), dma((1 + HALVES,)),
            pltpu.SemaphoreType.REGULAR((n_z // 2 - 1,)), pltpu.SemaphoreType.REGULAR((n_z // 2 - 1,)),
            dma((len(operands) - 1,)), dma((FETCH,)),
            dma, dma,
            dma((HALVES,)), dma((HALVES,)),
            dma((HALVES,)), dma((HALVES, PARTS)),
            dma((HALVES,)), dma((HALVES,)),
            dma, dma((HALVES, PARTS)),
            dma((HALVES,)), dma((HALVES,)),
            dma((HALVES,)), dma((HALVES,)),
        ],
        compiler_params=pltpu.CompilerParams(
            collective_id=0, has_side_effects=True, vmem_limit_bytes=62 * 2**20),
        name="layer",
    )(*operands)
    return pl.pallas_call(
        hand_over,
        out_shape=tuple(jax.ShapeDtypeStruct(o.shape, o.dtype) for o in outs),
        in_specs=[hbm, hbm],
        out_specs=(hbm, hbm),
        scratch_shapes=[pltpu.VMEM(o.shape, o.dtype) for o in outs] + [dma((5,)), dma((5,))],
        compiler_params=pltpu.CompilerParams(vmem_limit_bytes=62 * 2**20),
        name="hand_over",
    )(*outs)


def solution(mesh):
    both = ("grp", "mem")
    in_specs = (
        P(both, None), P(both), P(both, None, None), P(both), P(both), P(both),
        P(both, None), P(both), P(), P(),
    )
    out_specs = (P(both, None), P(both, None))
    fn = functools.partial(body, mesh.shape["grp"], mesh.shape["mem"])
    return jax.shard_map(fn, mesh=mesh, in_specs=in_specs, out_specs=out_specs, check_vma=False)
```

```python
import functools

import jax
import jax.numpy as jnp
from jax import lax
from jax.experimental import pallas as pl
from jax.experimental.pallas import tpu as pltpu
from jax.sharding import PartitionSpec as P

MESH = pl.DeviceIdType.MESH
NX = 4
NC = 2
LANE = 128
HALVES = 2
PARTS = 6
FETCH = 4


def log2(n):
    assert n & (n - 1) == 0
    return n.bit_length() - 1


def kernel(
    n_grp, n_mem, trow_h, tcol_h, src_h, deg_h, tiles_h, ids_h, mrow_h, mdeg_h, w1_h, w2_h, newm, mirror,
    trow, tcol, src, deg, tiles, idin, mrow, mdeg, w1, w2,
    scaled, bits, lhs, rhs, part, place, idrecv, even, odd, put, take, precv, col, xacc, xrecv, zsend, zrecv, table, served,
    up_s, down_s, in_s, tile_s, id_s, id_r, y_s, y_r, x_s, x_r, z_s, z_r, gz_s, gz_r, gx_s, gx_r, b_s, b_r,
):
    g = lax.axis_index("grp")
    m = lax.axis_index("mem")
    n_z, n_y = n_grp // NX, n_mem // NC
    x, z = lax.rem(g, NX), g // NX
    c, y = lax.rem(m, NC), m // NC
    tile = tiles.shape[1]
    n_tiles = tiles.shape[0]
    slot_total = precv.shape[1]
    slots = slot_total // n_mem
    owned = mrow.shape[0]
    half_z = n_z // 2
    z_part = n_z // PARTS
    rows = z_part * owned

    def mem_of(dy, dc):
        return lax.rem(y + dy + n_y, n_y) * NC + lax.rem(c + dc, NC)

    def grp_x(j):
        return z * NX + lax.rem(x + j + NX, NX)

    def grp_z(k):
        return lax.rem(z + k + n_z, n_z) * NX + x

    def pos(k):
        return 2 * abs(k - half_z) - (1 if k < half_z else 0)

    y_order = [0] + [s for d in range(1, n_y // 2) for s in (n_y - d, d)] + [n_y // 2]
    mem_order = [(dy, dc) for dy in reversed(y_order) for dc in range(NC) if (dy, dc) != (0, 0)]
    x_order = sorted(range(1, NX), key=lambda j: -min(j, NX - j))
    z_order = sorted(range(1, n_z), key=pos)

    fetch = [
        pltpu.make_async_copy(a, b, in_s.at[i])
        for i, (a, b) in enumerate([
            (deg_h, deg), (src_h, src), (trow_h, trow), (tcol_h, tcol), (ids_h, idin),
            (mrow_h, mrow), (mdeg_h, mdeg), (w1_h, w1), (w2_h, w2)])
    ]
    step = n_tiles // FETCH
    fetch_tiles = [
        pltpu.make_async_copy(tiles_h.at[pl.ds(i * step, step)], tiles.at[pl.ds(i * step, step)], tile_s.at[i])
        for i in range(FETCH)
    ]
    for copy in fetch[:5]:
        copy.start()
    for copy in fetch_tiles:
        copy.start()
    for copy in fetch[5:]:
        copy.start()

    barrier = pltpu.get_barrier_semaphore()
    partners = [(g, mem_of(*d)) for d in mem_order] + [(grp_x(j), m) for j in x_order] + [
        (grp_z(k), m) for k in (1, n_z - 1)]
    for who in partners:
        pl.semaphore_signal(barrier, inc=1, device_id=who, device_id_type=MESH)

    fetch[0].wait()
    fetch[1].wait()
    scale = lax.rsqrt(deg[...].astype(jnp.float32))
    for k in range(src.shape[0] // tile):
        column = jnp.broadcast_to(scale[k : k + 1, :], (tile, tile)).T
        for h in range(HALVES):
            at = (pl.ds(k * tile, tile), pl.ds(h * LANE, LANE))
            scaled[h, k] = (src[at].astype(jnp.float32) * column).astype(jnp.bfloat16)
    for copy in fetch[2:5]:
        copy.wait()

    ids = idin[...]
    group = jnp.right_shift(ids, log2(owned * n_mem))
    dx = jnp.bitwise_and(group, NX - 1) - x
    dx = jnp.where(dx < 0, dx + NX, dx)
    dz = jnp.right_shift(group, log2(NX)) - z
    dz = jnp.where(dz < 0, dz + n_z, dz)
    order = 2 * jnp.abs(dz - half_z) - jnp.where(dz < half_z, 1, 0)
    z_group = jnp.right_shift(order, log2(z_part))
    spots = (z_group * NX + dx) * rows + jnp.bitwise_and(order, z_part - 1) * owned + jnp.bitwise_and(
        ids, owned - 1)

    for k in range(n_y):
        place[k] = spots[k : k + 1, :]

    def fill_rhs(h):
        for t in range(n_tiles):
            rhs[h, t * tile : (t + 1) * tile, :] = scaled[h, tcol[t]]

    fill_rhs(0)
    for i in range(FETCH):
        fetch_tiles[i].wait()
        for t in range(i * step, (i + 1) * step):
            bits[t] = tiles[t].astype(jnp.float32).astype(jnp.bfloat16)

    def sums_for(h, dy):
        block = lax.rem(y + dy, n_y)
        if h == 0:
            for t in range(n_tiles):
                edges = bits[t]
                lhs[dy, :, t * tile : (t + 1) * tile] = jnp.where(trow[t] == block, edges, jnp.zeros_like(edges))
        part[h, dy] = jnp.dot(lhs[dy], rhs[h], preferred_element_type=jnp.float32).astype(jnp.bfloat16)


    def slot_of(dy, dc):
        return dy * NC + dc

    def id_copy(dy, dc):
        return pltpu.make_async_remote_copy(
            src_ref=place.at[lax.rem(y + dy, n_y)], dst_ref=idrecv.at[slot_of(dy, dc)], send_sem=id_s, recv_sem=id_r,
            device_id=(g, mem_of(dy, dc)), device_id_type=MESH)

    def y_copy(h, dy, dc):
        to = mem_of(dy, dc)
        return pltpu.make_async_remote_copy(
            src_ref=part.at[h, dy, pl.ds(pl.multiple_of(lax.rem(to, NC) * slots, slots), slots)],
            dst_ref=precv.at[h, pl.ds(slot_of(dy, dc) * slots, slots)],
            send_sem=y_s.at[h], recv_sem=y_r.at[h], device_id=(g, to), device_id_type=MESH)

    def x_copy(h, q, j):
        return pltpu.make_async_remote_copy(
            src_ref=col.at[h, q, j], dst_ref=xrecv.at[h, q, j], send_sem=x_s.at[h], recv_sem=x_r.at[h, q],
            device_id=(grp_x(j), m), device_id_type=MESH)

    def z_copy(h, k):
        return pltpu.make_async_remote_copy(
            src_ref=zsend.at[h, pos(k)], dst_ref=zrecv.at[h, k], send_sem=z_s.at[h], recv_sem=z_r.at[h],
            device_id=(grp_z(k), m), device_id_type=MESH)

    def z_rows(k):
        return pos(k) // z_part, pl.ds(pos(k) % z_part * owned, owned)

    def gz_copy(h, k):
        q, at = z_rows(0)
        to_q, to_at = z_rows((n_z - k) % n_z)
        return pltpu.make_async_remote_copy(
            src_ref=table.at[h, q, 0, at], dst_ref=table.at[h, to_q, 0, to_at], send_sem=gz_s,
            recv_sem=gz_r.at[h, to_q], device_id=(grp_z(k), m), device_id_type=MESH)

    def gx_copy(h, q, j):
        return pltpu.make_async_remote_copy(
            src_ref=table.at[h, q, 0], dst_ref=table.at[h, q, NX - j], send_sem=gx_s.at[h], recv_sem=gx_r.at[h],
            device_id=(grp_x(j), m), device_id_type=MESH)

    def b_copy(h, dy, dc):
        to = mem_of(-dy, dc)
        return pltpu.make_async_remote_copy(
            src_ref=served.at[h, pl.ds(slot_of(dy, dc) * slots, slots)],
            dst_ref=mirror.at[pl.ds(pl.multiple_of(m * slots, slots), slots), pl.ds(h * LANE, LANE)],
            send_sem=b_s.at[h], recv_sem=b_r.at[h], device_id=(g, to), device_id_type=MESH)

    def tell(r):
        if r < half_z - 1:
            pl.semaphore_signal(up_s.at[r], inc=1, device_id=(grp_z(1), m), device_id_type=MESH)
            pl.semaphore_signal(down_s.at[r], inc=1, device_id=(grp_z(n_z - 1), m), device_id_type=MESH)

    def hear(r):
        pl.semaphore_wait(up_s.at[r], 1)
        pl.semaphore_wait(down_s.at[r], 1)
        tell(r + 1)

    def drain(ref, sem):
        pltpu.make_async_copy(ref, ref, sem).wait()

    mine = pl.ds(pl.multiple_of(m * slots, slots), slots)
    idrecv[0] = place[y]
    for h in range(HALVES):
        if h:
            fill_rhs(h)
        for i, dy in enumerate(reversed(y_order)):
            sums_for(h, dy)
            if h == 0 and i == 0:
                pl.semaphore_wait(barrier, len(partners))
            for dc in range(NC):
                if (dy, dc) != (0, 0):
                    y_copy(h, dy, dc).start()
            if h == 0 and i == 0:
                tell(0)
            if h == 0 and i == 2:
                for d in mem_order:
                    id_copy(*d).start()
        precv[h, 0:slots] = part[h, 0, pl.ds(pl.multiple_of(c * slots, slots), slots), :]

    hear(0)
    drain(idrecv.at[pl.ds(1, n_mem - 1)], id_r)
    for k in range(n_y):
        even[k : k + 1, :] = idrecv[NC * k]
        odd[k : k + 1, :] = idrecv[NC * k + 1]
    lane = lax.broadcasted_iota(jnp.int32, (n_y, LANE), 1)
    low = jnp.where(c == 0, even[...], pltpu.roll(even[...], slots, 1))
    high = jnp.where(c == 0, pltpu.roll(odd[...], slots, 1), odd[...])
    spot = jnp.where(lane < slots, low, high)
    n_table = PARTS * NX * rows
    even[...] = spot

    def build_put(v, carry):
        row = lax.broadcasted_iota(jnp.int32, (LANE, LANE), 0) + v * LANE
        for k in range(n_y):
            put[pl.ds(pl.multiple_of(v * LANE, LANE), LANE), k * LANE : (k + 1) * LANE] = jnp.where(
                row == even[k : k + 1, :], 1.0, 0.0).astype(jnp.bfloat16)
        return carry

    lax.fori_loop(0, n_table // LANE, build_put, 0)

    hear(1)

    group_rows = NX * rows
    for h in range(HALVES):
        drain(precv.at[h, pl.ds(slots, slot_total - slots)], y_r.at[h])
        for q in range(PARTS):
            block = jnp.dot(put[q * group_rows : (q + 1) * group_rows, :], precv[h], preferred_element_type=jnp.float32)
            for j in x_order:
                col[h, q, j] = block[j * rows : (j + 1) * rows].astype(jnp.bfloat16)
                x_copy(h, q, j).start()
            xacc[h, q] = block[0:rows]
        if h == 0:
            for r in range(2, half_z - 1):
                hear(r)

    for h in range(HALVES):
        for q in range(PARTS):
            drain(xrecv.at[h, q, pl.ds(1, NX - 1)], x_r.at[h, q])
            total = xacc[h, q]
            for j in range(1, NX):
                total = total + xrecv[h, q, j].astype(jnp.float32)
            xacc[h, q] = total
            for i in range(z_part):
                zsend[h, q * z_part + i] = total[i * owned : (i + 1) * owned].astype(jnp.bfloat16)
            for k in z_order:
                if pos(k) // z_part == q:
                    z_copy(h, k).start()

    def build_take(k, carry):
        column = jnp.broadcast_to(even[pl.ds(k, 1), :], (LANE, LANE)).T
        for v in range(n_table // LANE):
            row = lax.broadcasted_iota(jnp.int32, (LANE, LANE), 1) + v * LANE
            take[pl.ds(pl.multiple_of(k * LANE, LANE), LANE), v * LANE : (v + 1) * LANE] = jnp.where(
                column == row, 1.0, 0.0).astype(jnp.bfloat16)
        return carry

    lax.fori_loop(0, n_y, build_take, 0)
    for copy in fetch[5:]:
        copy.wait()
    drain(idrecv.at[pl.ds(1, n_mem - 1)], id_s)
    for h in range(HALVES):
        drain(precv.at[h, pl.ds(slots, slot_total - slots)], y_s.at[h])
        drain(xrecv.at[h, :, pl.ds(1, NX - 1)], x_s.at[h])

    own_q, own_at = z_rows(0)
    sums = []
    for h in range(HALVES):
        drain(zrecv.at[h, pl.ds(1, n_z - 1)], z_r.at[h])
        total = xacc[h, own_q, own_at, :]
        for k in range(1, n_z):
            total = total + zrecv[h, k].astype(jnp.float32)
        sums.append(total)

    scale = lax.rsqrt(mdeg[...].astype(jnp.float32))
    diagonal = lax.broadcasted_iota(jnp.int32, (owned, owned), 0) == lax.broadcasted_iota(
        jnp.int32, (owned, owned), 1)
    scale = jnp.sum(jnp.where(diagonal, jnp.broadcast_to(scale, (owned, owned)), 0.0), axis=1, keepdims=True)
    neigh = jnp.concatenate(sums, axis=1) * scale
    embed = mrow[...].astype(jnp.float32)
    first = (embed + neigh).astype(jnp.bfloat16)
    second = (neigh * embed).astype(jnp.bfloat16)
    result = jnp.dot(first, w1[...], preferred_element_type=jnp.float32) + jnp.dot(
        second, w2[...], preferred_element_type=jnp.float32)
    new = jnp.where(result > 0, result, 0.2 * result).astype(jnp.bfloat16)
    for h in range(HALVES):
        table[h, own_q, 0, own_at, :] = new[:, h * LANE : (h + 1) * LANE]

    for k in reversed(z_order):
        gz_copy(0, k).start()
    newm[...] = new
    for h in range(HALVES):
        for q in reversed(range(PARTS)):
            n_here = z_part - (1 if q == own_q else 0)
            drain(table.at[h, q, 0, pl.ds(0, n_here * owned)], gz_r.at[h, q])
            for j in x_order:
                gx_copy(h, q, j).start()
            if (h, q) == (0, PARTS // 2):
                for k in reversed(z_order):
                    gz_copy(1, k).start()

    for h in range(HALVES):
        drain(table.at[h, :, pl.ds(1, NX - 1)], gx_r.at[h])
        for first in (4, 2, 6, 0):
            at = slice(first * LANE, (first + 2) * LANE)
            served[h, at, :] = jnp.dot(
                take[at, :], table[h].reshape(n_table, LANE), preferred_element_type=jnp.float32
            ).astype(jnp.bfloat16)
            for d in mem_order:
                if d[0] // 2 * 2 == first:
                    b_copy(h, *d).start()
        mirror[mine, h * LANE : (h + 1) * LANE] = served[h, 0:slots, :]

    drain(zrecv.at[:, pl.ds(1, n_z - 1)], gz_s)
    for h in range(HALVES):
        drain(zrecv.at[h, pl.ds(1, n_z - 1)], z_s.at[h])
        drain(table.at[h, :, pl.ds(1, NX - 1)], gx_s.at[h])
    for h in range(HALVES):
        drain(served.at[h, pl.ds(slots, slot_total - slots)], b_s.at[h])
        drain(served.at[h, pl.ds(slots, slot_total - slots)], b_r.at[h])


def hand_over(new_in, mirror_in, new_out, mirror_out, sems):
    copies = [
        pltpu.make_async_copy(mirror_in, mirror_out, sems.at[0]),
        pltpu.make_async_copy(new_in, new_out, sems.at[1]),
    ]
    for copy in copies:
        copy.start()
    for copy in copies:
        copy.wait()


def body(n_grp, n_mem, source_rows, source_degree, edge_tiles, tile_row, tile_col, mirror_ids,
         master_rows, master_degree, weight_one, weight_two):
    n_tiles, tile, _ = edge_tiles.shape
    src_dev, width = source_rows.shape
    slot_total = mirror_ids.shape[0]
    owned = master_rows.shape[0]
    n_z = n_grp // NX
    z_part = n_z // PARTS
    rows = z_part * owned
    n_table = n_z * NX * owned
    hbm = pl.BlockSpec(memory_space=pltpu.HBM)
    vmem = pl.BlockSpec(memory_space=pltpu.VMEM)
    bf, f32, i32 = jnp.bfloat16, jnp.float32, jnp.int32
    dma = pltpu.SemaphoreType.DMA
    operands = (
        tile_row, tile_col, source_rows, source_degree.reshape(-1, tile), edge_tiles, mirror_ids.reshape(-1, LANE),
        master_rows, master_degree.reshape(1, owned), weight_one, weight_two,
    )
    operands = [pltpu.with_memory_space_constraint(a, pltpu.HBM) for a in operands]
    outs = pl.pallas_call(
        functools.partial(kernel, n_grp, n_mem),
        out_shape=(
            pltpu.VMEM((owned, width), bf),
            pltpu.VMEM((slot_total, width), bf),
        ),
        in_specs=[hbm] * len(operands),
        out_specs=(vmem, vmem),
        scratch_shapes=[
            pltpu.SMEM((n_tiles,), i32),
            pltpu.SMEM((n_tiles,), i32),
            pltpu.VMEM((src_dev, width), bf),
            pltpu.VMEM((src_dev // tile, tile), i32),
            pltpu.VMEM((n_tiles, tile, tile), i32),
            pltpu.VMEM((slot_total // LANE, LANE), i32),
            pltpu.VMEM((owned, width), bf),
            pltpu.VMEM((1, owned), i32),
            pltpu.VMEM((width, width), bf),
            pltpu.VMEM((width, width), bf),
            pltpu.VMEM((HALVES, src_dev // tile, tile, LANE), bf),
            pltpu.VMEM((n_tiles, tile, tile), bf),
            pltpu.VMEM((n_mem // NC, tile, n_tiles * tile), bf),
            pltpu.VMEM((HALVES, n_tiles * tile, LANE), bf),
            pltpu.VMEM((HALVES, n_mem // NC, tile, LANE), bf),
            pltpu.VMEM((n_mem // NC, 1, LANE), i32),
            pltpu.VMEM((n_mem, 1, LANE), i32),
            pltpu.VMEM((slot_total // LANE, LANE), i32),
            pltpu.VMEM((slot_total // LANE, LANE), i32),
            pltpu.VMEM((n_table, slot_total), bf),
            pltpu.VMEM((slot_total, n_table), bf),
            pltpu.VMEM((HALVES, slot_total, LANE), bf),
            pltpu.VMEM((HALVES, PARTS, NX, rows, LANE), bf),
            pltpu.VMEM((HALVES, PARTS, rows, LANE), f32),
            pltpu.VMEM((HALVES, PARTS, NX, rows, LANE), bf),
            pltpu.VMEM((HALVES, n_z, owned, LANE), bf),
            pltpu.VMEM((HALVES, n_z, owned, LANE), bf),
            pltpu.VMEM((HALVES, PARTS, NX, rows, LANE), bf),
            pltpu.VMEM((HALVES, slot_total, LANE), bf),
            pltpu.SemaphoreType.REGULAR((n_z // 2 - 1,)), pltpu.SemaphoreType.REGULAR((n_z // 2 - 1,)),
            dma((len(operands) - 1,)), dma((FETCH,)),
            dma, dma,
            dma((HALVES,)), dma((HALVES,)),
            dma((HALVES,)), dma((HALVES, PARTS)),
            dma((HALVES,)), dma((HALVES,)),
            dma, dma((HALVES, PARTS)),
            dma((HALVES,)), dma((HALVES,)),
            dma((HALVES,)), dma((HALVES,)),
        ],
        compiler_params=pltpu.CompilerParams(
            collective_id=0, has_side_effects=True, vmem_limit_bytes=40 * 2**20),
        name="layer",
    )(*operands)
    return pl.pallas_call(
        hand_over,
        out_shape=tuple(jax.ShapeDtypeStruct(o.shape, o.dtype) for o in outs),
        in_specs=[vmem, vmem],
        out_specs=(hbm, hbm),
        scratch_shapes=[dma((2,))],
        compiler_params=pltpu.CompilerParams(vmem_limit_bytes=16 * 2**20),
        name="hand_over",
    )(*outs)


def solution(mesh):
    both = ("grp", "mem")
    in_specs = (
        P(both, None), P(both), P(both, None, None), P(both), P(both), P(both),
        P(both, None), P(both), P(), P(),
    )
    out_specs = (P(both, None), P(both, None))
    fn = functools.partial(body, mesh.shape["grp"], mesh.shape["mem"])
    return jax.shard_map(fn, mesh=mesh, in_specs=in_specs, out_specs=out_specs, check_vma=False)
```

```python
import functools

import jax
import jax.numpy as jnp
from jax import lax
from jax.experimental import pallas as pl
from jax.experimental.pallas import tpu as pltpu
from jax.sharding import PartitionSpec as P

MESH = pl.DeviceIdType.MESH
NX = 4
NC = 2
LANE = 128
HALVES = 2
PARTS = 6
FETCH = 4


def log2(n):
    assert n & (n - 1) == 0
    return n.bit_length() - 1


def kernel(
    n_grp, n_mem, trow_h, tcol_h, src_h, deg_h, tiles_h, ids_h, mrow_h, mdeg_h, w1_h, w2_h, newm, mirror,
    trow, tcol, src, deg, tiles, idin, mrow, mdeg, w1, w2,
    scaled, bits, lhs, rhs, part, place, idrecv, even, odd, put, take, precv, col, xacc, xrecv, zsend, zrecv, table, served,
    up_s, down_s, in_s, tile_s, id_s, id_r, y_s, y_r, x_s, x_r, z_s, z_r, gz_s, gz_r, gx_s, gx_r, b_s, b_r,
):
    g = lax.axis_index("grp")
    m = lax.axis_index("mem")
    n_z, n_y = n_grp // NX, n_mem // NC
    x, z = lax.rem(g, NX), g // NX
    c, y = lax.rem(m, NC), m // NC
    tile = tiles.shape[1]
    n_tiles = tiles.shape[0]
    slot_total = precv.shape[1]
    slots = slot_total // n_mem
    owned = mrow.shape[0]
    half_z = n_z // 2
    z_part = n_z // PARTS
    rows = z_part * owned

    def mem_of(dy, dc):
        return lax.rem(y + dy + n_y, n_y) * NC + lax.rem(c + dc, NC)

    def grp_x(j):
        return z * NX + lax.rem(x + j + NX, NX)

    def grp_z(k):
        return lax.rem(z + k + n_z, n_z) * NX + x

    def pos(k):
        return 2 * abs(k - half_z) - (1 if k < half_z else 0)

    y_order = [0] + [s for d in range(1, n_y // 2) for s in (n_y - d, d)] + [n_y // 2]
    mem_order = [(dy, dc) for dy in reversed(y_order) for dc in range(NC) if (dy, dc) != (0, 0)]
    x_order = sorted(range(1, NX), key=lambda j: -min(j, NX - j))
    z_order = sorted(range(1, n_z), key=pos)

    fetch = [
        pltpu.make_async_copy(a, b, in_s.at[i])
        for i, (a, b) in enumerate([
            (deg_h, deg), (src_h, src), (trow_h, trow), (tcol_h, tcol), (ids_h, idin),
            (mrow_h, mrow), (mdeg_h, mdeg), (w1_h, w1), (w2_h, w2)])
    ]
    step = n_tiles // FETCH
    fetch_tiles = [
        pltpu.make_async_copy(tiles_h.at[pl.ds(i * step, step)], tiles.at[pl.ds(i * step, step)], tile_s.at[i])
        for i in range(FETCH)
    ]
    for copy in fetch[:5]:
        copy.start()
    for copy in fetch_tiles:
        copy.start()
    for copy in fetch[5:]:
        copy.start()

    barrier = pltpu.get_barrier_semaphore()
    partners = [(g, mem_of(*d)) for d in mem_order] + [(grp_x(j), m) for j in x_order] + [
        (grp_z(k), m) for k in (1, n_z - 1)]
    for who in partners:
        pl.semaphore_signal(barrier, inc=1, device_id=who, device_id_type=MESH)

    fetch[0].wait()
    fetch[1].wait()
    scale = lax.rsqrt(deg[...].astype(jnp.float32))
    columns = [
        jnp.broadcast_to(scale[k : k + 1, :], (tile, tile)).T for k in range(src.shape[0] // tile)]
    for copy in fetch[2:5]:
        copy.wait()

    def fill_rhs(h):
        for k, column in enumerate(columns):
            at = (pl.ds(k * tile, tile), pl.ds(h * LANE, LANE))
            scaled[h, k] = (src[at].astype(jnp.float32) * column).astype(jnp.bfloat16)
        for t in range(n_tiles):
            rhs[h, t * tile : (t + 1) * tile, :] = scaled[h, tcol[t]]

    fill_rhs(0)
    for i in range(FETCH):
        fetch_tiles[i].wait()
        for t in range(i * step, (i + 1) * step):
            bits[t] = tiles[t].astype(jnp.float32).astype(jnp.bfloat16)

    def find_places():
        ids = idin[...]
        group = jnp.right_shift(ids, log2(owned * n_mem))
        dx = jnp.bitwise_and(group, NX - 1) - x
        dx = jnp.where(dx < 0, dx + NX, dx)
        dz = jnp.right_shift(group, log2(NX)) - z
        dz = jnp.where(dz < 0, dz + n_z, dz)
        order = 2 * jnp.abs(dz - half_z) - jnp.where(dz < half_z, 1, 0)
        z_group = jnp.right_shift(order, log2(z_part))
        spots = (z_group * NX + dx) * rows + jnp.bitwise_and(order, z_part - 1) * owned + jnp.bitwise_and(
            ids, owned - 1)

        for k in range(n_y):
            place[k] = spots[k : k + 1, :]

    def sums_for(h, dy):
        block = lax.rem(y + dy, n_y)
        if h == 0:
            for t in range(n_tiles):
                edges = bits[t]
                lhs[dy, :, t * tile : (t + 1) * tile] = jnp.where(trow[t] == block, edges, jnp.zeros_like(edges))
        part[h, dy] = jnp.dot(lhs[dy], rhs[h], preferred_element_type=jnp.float32).astype(jnp.bfloat16)


    def slot_of(dy, dc):
        return dy * NC + dc

    def id_copy(dy, dc):
        return pltpu.make_async_remote_copy(
            src_ref=place.at[lax.rem(y + dy, n_y)], dst_ref=idrecv.at[slot_of(dy, dc)], send_sem=id_s, recv_sem=id_r,
            device_id=(g, mem_of(dy, dc)), device_id_type=MESH)

    def y_copy(h, dy, dc):
        to = mem_of(dy, dc)
        return pltpu.make_async_remote_copy(
            src_ref=part.at[h, dy, pl.ds(pl.multiple_of(lax.rem(to, NC) * slots, slots), slots)],
            dst_ref=precv.at[h, pl.ds(slot_of(dy, dc) * slots, slots)],
            send_sem=y_s.at[h], recv_sem=y_r.at[h], device_id=(g, to), device_id_type=MESH)

    def x_copy(h, q, j):
        return pltpu.make_async_remote_copy(
            src_ref=col.at[h, q, j], dst_ref=xrecv.at[h, q, j], send_sem=x_s.at[h], recv_sem=x_r.at[h, q],
            device_id=(grp_x(j), m), device_id_type=MESH)

    def z_copy(h, k):
        return pltpu.make_async_remote_copy(
            src_ref=zsend.at[h, pos(k)], dst_ref=zrecv.at[h, k], send_sem=z_s.at[h], recv_sem=z_r.at[h],
            device_id=(grp_z(k), m), device_id_type=MESH)

    def z_rows(k):
        return pos(k) // z_part, pl.ds(pos(k) % z_part * owned, owned)

    def gz_copy(h, k):
        q, at = z_rows(0)
        to_q, to_at = z_rows((n_z - k) % n_z)
        return pltpu.make_async_remote_copy(
            src_ref=table.at[h, q, 0, at], dst_ref=table.at[h, to_q, 0, to_at], send_sem=gz_s,
            recv_sem=gz_r.at[h, to_q], device_id=(grp_z(k), m), device_id_type=MESH)

    def gx_copy(h, q, j):
        return pltpu.make_async_remote_copy(
            src_ref=table.at[h, q, 0], dst_ref=table.at[h, q, NX - j], send_sem=gx_s.at[h], recv_sem=gx_r.at[h],
            device_id=(grp_x(j), m), device_id_type=MESH)

    def b_copy(h, dy, dc):
        to = mem_of(-dy, dc)
        return pltpu.make_async_remote_copy(
            src_ref=served.at[h, pl.ds(slot_of(dy, dc) * slots, slots)],
            dst_ref=mirror.at[pl.ds(pl.multiple_of(m * slots, slots), slots), pl.ds(h * LANE, LANE)],
            send_sem=b_s.at[h], recv_sem=b_r.at[h], device_id=(g, to), device_id_type=MESH)

    def tell(r):
        if r < half_z - 1:
            pl.semaphore_signal(up_s.at[r], inc=1, device_id=(grp_z(1), m), device_id_type=MESH)
            pl.semaphore_signal(down_s.at[r], inc=1, device_id=(grp_z(n_z - 1), m), device_id_type=MESH)

    def hear(r):
        pl.semaphore_wait(up_s.at[r], 1)
        pl.semaphore_wait(down_s.at[r], 1)
        tell(r + 1)

    def drain(ref, sem):
        pltpu.make_async_copy(ref, ref, sem).wait()

    mine = pl.ds(pl.multiple_of(m * slots, slots), slots)
    for h in range(HALVES):
        if h:
            fill_rhs(h)
        for i, dy in enumerate(reversed(y_order)):
            sums_for(h, dy)
            if h == 0 and i == 0:
                pl.semaphore_wait(barrier, len(partners))
            for dc in range(NC):
                if (dy, dc) != (0, 0):
                    y_copy(h, dy, dc).start()
            if h == 0 and i == 0:
                tell(0)
            if h == 0 and i == 2:
                find_places()
                for d in mem_order:
                    id_copy(*d).start()
        precv[h, 0:slots] = part[h, 0, pl.ds(pl.multiple_of(c * slots, slots), slots), :]

    hear(0)
    drain(idrecv.at[pl.ds(1, n_mem - 1)], id_r)
    idrecv[0] = place[y]
    for k in range(n_y):
        even[k : k + 1, :] = idrecv[NC * k]
        odd[k : k + 1, :] = idrecv[NC * k + 1]
    lane = lax.broadcasted_iota(jnp.int32, (n_y, LANE), 1)
    low = jnp.where(c == 0, even[...], pltpu.roll(even[...], slots, 1))
    high = jnp.where(c == 0, pltpu.roll(odd[...], slots, 1), odd[...])
    spot = jnp.where(lane < slots, low, high)
    n_table = PARTS * NX * rows
    even[...] = spot

    def build_put(v, carry):
        row = lax.broadcasted_iota(jnp.int32, (LANE, LANE), 0) + v * LANE
        for k in range(n_y):
            put[pl.ds(pl.multiple_of(v * LANE, LANE), LANE), k * LANE : (k + 1) * LANE] = jnp.where(
                row == even[k : k + 1, :], 1.0, 0.0).astype(jnp.bfloat16)
        return carry

    lax.fori_loop(0, n_table // LANE, build_put, 0)

    hear(1)

    def rest_of_x(h, first, last):
        for q in range(first, last):
            drain(xrecv.at[h, q, pl.ds(1, NX - 1)], x_r.at[h, q])
            total = xacc[h, q]
            for j in range(1, NX):
                total = total + xrecv[h, q, j].astype(jnp.float32)
            xacc[h, q] = total
            for i in range(z_part):
                zsend[h, q * z_part + i] = total[i * owned : (i + 1) * owned].astype(jnp.bfloat16)
            for k in z_order:
                if pos(k) // z_part == q:
                    z_copy(h, k).start()

    group_rows = NX * rows
    for h in range(HALVES):
        drain(precv.at[h, pl.ds(slots, slot_total - slots)], y_r.at[h])
        for q in range(PARTS):
            block = jnp.dot(put[q * group_rows : (q + 1) * group_rows, :], precv[h], preferred_element_type=jnp.float32)
            for j in x_order:
                col[h, q, j] = block[j * rows : (j + 1) * rows].astype(jnp.bfloat16)
                x_copy(h, q, j).start()
            xacc[h, q] = block[0:rows]
        if h == 0:
            for r in range(2, half_z - 1):
                hear(r)
            rest_of_x(0, 0, PARTS // 3)

    rest_of_x(0, PARTS // 3, PARTS)
    rest_of_x(1, 0, PARTS)

    def build_take(k, carry):
        column = jnp.broadcast_to(even[pl.ds(k, 1), :], (LANE, LANE)).T
        for v in range(n_table // LANE):
            row = lax.broadcasted_iota(jnp.int32, (LANE, LANE), 1) + v * LANE
            take[pl.ds(pl.multiple_of(k * LANE, LANE), LANE), v * LANE : (v + 1) * LANE] = jnp.where(
                column == row, 1.0, 0.0).astype(jnp.bfloat16)
        return carry

    lax.fori_loop(0, n_y, build_take, 0)
    for copy in fetch[5:]:
        copy.wait()
    drain(idrecv.at[pl.ds(1, n_mem - 1)], id_s)
    for h in range(HALVES):
        drain(precv.at[h, pl.ds(slots, slot_total - slots)], y_s.at[h])
        drain(xrecv.at[h, :, pl.ds(1, NX - 1)], x_s.at[h])

    own_q, own_at = z_rows(0)
    sums = []
    for h in range(HALVES):
        drain(zrecv.at[h, pl.ds(1, n_z - 1)], z_r.at[h])
        total = xacc[h, own_q, own_at, :]
        for k in range(1, n_z):
            total = total + zrecv[h, k].astype(jnp.float32)
        sums.append(total)

    scale = lax.rsqrt(mdeg[...].astype(jnp.float32))
    diagonal = lax.broadcasted_iota(jnp.int32, (owned, owned), 0) == lax.broadcasted_iota(
        jnp.int32, (owned, owned), 1)
    scale = jnp.sum(jnp.where(diagonal, jnp.broadcast_to(scale, (owned, owned)), 0.0), axis=1, keepdims=True)
    neigh = jnp.concatenate(sums, axis=1) * scale
    embed = mrow[...].astype(jnp.float32)
    first = (embed + neigh).astype(jnp.bfloat16)
    second = (neigh * embed).astype(jnp.bfloat16)
    result = jnp.dot(first, w1[...], preferred_element_type=jnp.float32) + jnp.dot(
        second, w2[...], preferred_element_type=jnp.float32)
    new = jnp.where(result > 0, result, 0.2 * result).astype(jnp.bfloat16)
    for h in range(HALVES):
        table[h, own_q, 0, own_at, :] = new[:, h * LANE : (h + 1) * LANE]

    for k in z_order[:3] + z_order[:2:-1]:
        gz_copy(0, k).start()
    newm[...] = new
    for h in range(HALVES):
        for q in reversed(range(PARTS)):
            n_here = z_part - (1 if q == own_q else 0)
            drain(table.at[h, q, 0, pl.ds(0, n_here * owned)], gz_r.at[h, q])
            for j in x_order:
                gx_copy(h, q, j).start()
            if (h, q) == (0, PARTS // 2):
                for k in reversed(z_order):
                    gz_copy(1, k).start()

    for h in range(HALVES):
        drain(table.at[h, :, pl.ds(1, NX - 1)], gx_r.at[h])
        for first in (4, 2, 6, 0):
            at = slice(first * LANE, (first + 2) * LANE)
            served[h, at, :] = jnp.dot(
                take[at, :], table[h].reshape(n_table, LANE), preferred_element_type=jnp.float32
            ).astype(jnp.bfloat16)
            for d in mem_order:
                if d[0] // 2 * 2 == first:
                    b_copy(h, *d).start()
        mirror[mine, h * LANE : (h + 1) * LANE] = served[h, 0:slots, :]

    drain(zrecv.at[:, pl.ds(1, n_z - 1)], gz_s)
    for h in range(HALVES):
        drain(zrecv.at[h, pl.ds(1, n_z - 1)], z_s.at[h])
        drain(table.at[h, :, pl.ds(1, NX - 1)], gx_s.at[h])
    for h in range(HALVES):
        drain(served.at[h, pl.ds(slots, slot_total - slots)], b_s.at[h])
        drain(served.at[h, pl.ds(slots, slot_total - slots)], b_r.at[h])


def hand_over(new_in, mirror_in, new_out, mirror_out, sems):
    copies = [
        pltpu.make_async_copy(mirror_in, mirror_out, sems.at[0]),
        pltpu.make_async_copy(new_in, new_out, sems.at[1]),
    ]
    for copy in copies:
        copy.start()
    for copy in copies:
        copy.wait()


def body(n_grp, n_mem, source_rows, source_degree, edge_tiles, tile_row, tile_col, mirror_ids,
         master_rows, master_degree, weight_one, weight_two):
    n_tiles, tile, _ = edge_tiles.shape
    src_dev, width = source_rows.shape
    slot_total = mirror_ids.shape[0]
    owned = master_rows.shape[0]
    n_z = n_grp // NX
    z_part = n_z // PARTS
    rows = z_part * owned
    n_table = n_z * NX * owned
    hbm = pl.BlockSpec(memory_space=pltpu.HBM)
    vmem = pl.BlockSpec(memory_space=pltpu.VMEM)
    bf, f32, i32 = jnp.bfloat16, jnp.float32, jnp.int32
    dma = pltpu.SemaphoreType.DMA
    operands = (
        tile_row, tile_col, source_rows, source_degree.reshape(-1, tile), edge_tiles, mirror_ids.reshape(-1, LANE),
        master_rows, master_degree.reshape(1, owned), weight_one, weight_two,
    )
    operands = [pltpu.with_memory_space_constraint(a, pltpu.HBM) for a in operands]
    outs = pl.pallas_call(
        functools.partial(kernel, n_grp, n_mem),
        out_shape=(
            pltpu.VMEM((owned, width), bf),
            pltpu.VMEM((slot_total, width), bf),
        ),
        in_specs=[hbm] * len(operands),
        out_specs=(vmem, vmem),
        scratch_shapes=[
            pltpu.SMEM((n_tiles,), i32),
            pltpu.SMEM((n_tiles,), i32),
            pltpu.VMEM((src_dev, width), bf),
            pltpu.VMEM((src_dev // tile, tile), i32),
            pltpu.VMEM((n_tiles, tile, tile), i32),
            pltpu.VMEM((slot_total // LANE, LANE), i32),
            pltpu.VMEM((owned, width), bf),
            pltpu.VMEM((1, owned), i32),
            pltpu.VMEM((width, width), bf),
            pltpu.VMEM((width, width), bf),
            pltpu.VMEM((HALVES, src_dev // tile, tile, LANE), bf),
            pltpu.VMEM((n_tiles, tile, tile), bf),
            pltpu.VMEM((n_mem // NC, tile, n_tiles * tile), bf),
            pltpu.VMEM((HALVES, n_tiles * tile, LANE), bf),
            pltpu.VMEM((HALVES, n_mem // NC, tile, LANE), bf),
            pltpu.VMEM((n_mem // NC, 1, LANE), i32),
            pltpu.VMEM((n_mem, 1, LANE), i32),
            pltpu.VMEM((slot_total // LANE, LANE), i32),
            pltpu.VMEM((slot_total // LANE, LANE), i32),
            pltpu.VMEM((n_table, slot_total), bf),
            pltpu.VMEM((slot_total, n_table), bf),
            pltpu.VMEM((HALVES, slot_total, LANE), bf),
            pltpu.VMEM((HALVES, PARTS, NX, rows, LANE), bf),
            pltpu.VMEM((HALVES, PARTS, rows, LANE), f32),
            pltpu.VMEM((HALVES, PARTS, NX, rows, LANE), bf),
            pltpu.VMEM((HALVES, n_z, owned, LANE), bf),
            pltpu.VMEM((HALVES, n_z, owned, LANE), bf),
            pltpu.VMEM((HALVES, PARTS, NX, rows, LANE), bf),
            pltpu.VMEM((HALVES, slot_total, LANE), bf),
            pltpu.SemaphoreType.REGULAR((n_z // 2 - 1,)), pltpu.SemaphoreType.REGULAR((n_z // 2 - 1,)),
            dma((len(operands) - 1,)), dma((FETCH,)),
            dma, dma,
            dma((HALVES,)), dma((HALVES,)),
            dma((HALVES,)), dma((HALVES, PARTS)),
            dma((HALVES,)), dma((HALVES,)),
            dma, dma((HALVES, PARTS)),
            dma((HALVES,)), dma((HALVES,)),
            dma((HALVES,)), dma((HALVES,)),
        ],
        compiler_params=pltpu.CompilerParams(
            collective_id=0, has_side_effects=True, vmem_limit_bytes=40 * 2**20),
        name="layer",
    )(*operands)
    return pl.pallas_call(
        hand_over,
        out_shape=tuple(jax.ShapeDtypeStruct(o.shape, o.dtype) for o in outs),
        in_specs=[vmem, vmem],
        out_specs=(hbm, hbm),
        scratch_shapes=[dma((2,))],
        compiler_params=pltpu.CompilerParams(vmem_limit_bytes=16 * 2**20),
        name="hand_over",
    )(*outs)


def solution(mesh):
    both = ("grp", "mem")
    in_specs = (
        P(both, None), P(both), P(both, None, None), P(both), P(both), P(both),
        P(both, None), P(both), P(), P(),
    )
    out_specs = (P(both, None), P(both, None))
    fn = functools.partial(body, mesh.shape["grp"], mesh.shape["mem"])
    return jax.shard_map(fn, mesh=mesh, in_specs=in_specs, out_specs=out_specs, check_vma=False)
```

```python
import functools

import jax
import jax.numpy as jnp
from jax import lax
from jax.experimental import pallas as pl
from jax.experimental.pallas import tpu as pltpu
from jax.sharding import PartitionSpec as P

MESH = pl.DeviceIdType.MESH
NX = 4
NC = 2
LANE = 128
HALVES = 2
PARTS = 6
FETCH = 4


def log2(n):
    assert n & (n - 1) == 0
    return n.bit_length() - 1


def kernel(
    n_grp, n_mem, trow_h, tcol_h, src_h, deg_h, tiles_h, ids_h, mrow_h, mdeg_h, w1_h, w2_h, newm, mirror,
    trow, tcol, src, deg, tiles, idin, mrow, mdeg, w1, w2,
    scaled, bits, lhs, rhs, part, place, idrecv, even, odd, put, take, precv, col, xacc, xrecv, zsend, zrecv, table, served,
    up_s, down_s, in_s, tile_s, id_s, id_r, y_s, y_r, x_s, x_r, z_s, z_r, gz_s, gz_r, gx_s, gx_r, b_s, b_r,
):
    g = lax.axis_index("grp")
    m = lax.axis_index("mem")
    n_z, n_y = n_grp // NX, n_mem // NC
    x, z = lax.rem(g, NX), g // NX
    c, y = lax.rem(m, NC), m // NC
    tile = tiles.shape[1]
    n_tiles = tiles.shape[0]
    slot_total = precv.shape[1]
    slots = slot_total // n_mem
    owned = mrow.shape[0]
    half_z = n_z // 2
    z_part = n_z // PARTS
    rows = z_part * owned

    def mem_of(dy, dc):
        return lax.rem(y + dy + n_y, n_y) * NC + lax.rem(c + dc, NC)

    def grp_x(j):
        return z * NX + lax.rem(x + j + NX, NX)

    def grp_z(k):
        return lax.rem(z + k + n_z, n_z) * NX + x

    def pos(k):
        return 2 * abs(k - half_z) - (1 if k < half_z else 0)

    y_order = [0] + [s for d in range(1, n_y // 2) for s in (n_y - d, d)] + [n_y // 2]
    mem_order = [(dy, dc) for dy in reversed(y_order) for dc in range(NC) if (dy, dc) != (0, 0)]
    near = (1, n_y - 1, 0)
    x_order = sorted(range(1, NX), key=lambda j: -min(j, NX - j))
    z_order = sorted(range(1, n_z), key=pos)

    fetch = [
        pltpu.make_async_copy(a, b, in_s.at[i])
        for i, (a, b) in enumerate([
            (deg_h, deg), (src_h, src), (trow_h, trow), (tcol_h, tcol), (ids_h, idin),
            (mrow_h, mrow), (mdeg_h, mdeg), (w1_h, w1), (w2_h, w2)])
    ]
    step = n_tiles // FETCH
    fetch_tiles = [
        pltpu.make_async_copy(tiles_h.at[pl.ds(i * step, step)], tiles.at[pl.ds(i * step, step)], tile_s.at[i])
        for i in range(FETCH)
    ]
    barrier = pltpu.get_barrier_semaphore()
    partners = [(g, mem_of(*d)) for d in mem_order] + [(grp_x(j), m) for j in x_order] + [
        (grp_z(k), m) for k in (1, n_z - 1)]
    for who in partners:
        pl.semaphore_signal(barrier, inc=1, device_id=who, device_id_type=MESH)

    for copy in fetch[:2] + fetch_tiles + fetch[2:]:
        copy.start()

    fetch[0].wait()
    fetch[1].wait()
    scale = lax.rsqrt(deg[...].astype(jnp.float32))
    columns = [
        jnp.broadcast_to(scale[k : k + 1, :], (tile, tile)).T for k in range(src.shape[0] // tile)]
    for copy in fetch[2:5]:
        copy.wait()

    def fill_rhs(h):
        for k, column in enumerate(columns):
            at = (pl.ds(k * tile, tile), pl.ds(h * LANE, LANE))
            scaled[h, k] = (src[at].astype(jnp.float32) * column).astype(jnp.bfloat16)
        for t in range(n_tiles):
            rhs[h, t * tile : (t + 1) * tile, :] = scaled[h, tcol[t]]

    fill_rhs(0)
    for i in range(FETCH):
        fetch_tiles[i].wait()
        for t in range(i * step, (i + 1) * step):
            bits[t] = tiles[t].astype(jnp.float32).astype(jnp.bfloat16)

    def find_places():
        ids = idin[...]
        group = jnp.right_shift(ids, log2(owned * n_mem))
        dx = jnp.bitwise_and(group, NX - 1) - x
        dx = jnp.where(dx < 0, dx + NX, dx)
        dz = jnp.right_shift(group, log2(NX)) - z
        dz = jnp.where(dz < 0, dz + n_z, dz)
        order = 2 * jnp.abs(dz - half_z) - jnp.where(dz < half_z, 1, 0)
        z_group = jnp.right_shift(order, log2(z_part))
        spots = (z_group * NX + dx) * rows + jnp.bitwise_and(order, z_part - 1) * owned + jnp.bitwise_and(
            ids, owned - 1)

        for k in range(n_y):
            place[k] = spots[k : k + 1, :]

    def sums_for(h, dy):
        block = lax.rem(y + dy, n_y)
        if h == 0:
            for t in range(n_tiles):
                edges = bits[t]
                lhs[dy, :, t * tile : (t + 1) * tile] = jnp.where(trow[t] == block, edges, jnp.zeros_like(edges))
        part[h, dy] = jnp.dot(lhs[dy], rhs[h], preferred_element_type=jnp.float32).astype(jnp.bfloat16)


    def slot_of(dy, dc):
        return dy * NC + dc

    def id_copy(dy, dc):
        return pltpu.make_async_remote_copy(
            src_ref=place.at[lax.rem(y + dy, n_y)], dst_ref=idrecv.at[slot_of(dy, dc)], send_sem=id_s, recv_sem=id_r,
            device_id=(g, mem_of(dy, dc)), device_id_type=MESH)

    def y_copy(h, dy, dc):
        to = mem_of(dy, dc)
        return pltpu.make_async_remote_copy(
            src_ref=part.at[h, dy, pl.ds(pl.multiple_of(lax.rem(to, NC) * slots, slots), slots)],
            dst_ref=precv.at[h, pl.ds(slot_of(dy, dc) * slots, slots)],
            send_sem=y_s.at[h], recv_sem=y_r.at[h], device_id=(g, to), device_id_type=MESH)

    def x_copy(h, q, j):
        return pltpu.make_async_remote_copy(
            src_ref=col.at[h, q, j], dst_ref=xrecv.at[h, q, j], send_sem=x_s.at[h], recv_sem=x_r.at[h, q],
            device_id=(grp_x(j), m), device_id_type=MESH)

    def z_copy(h, k):
        return pltpu.make_async_remote_copy(
            src_ref=zsend.at[h, pos(k)], dst_ref=zrecv.at[h, k], send_sem=z_s.at[h], recv_sem=z_r.at[h],
            device_id=(grp_z(k), m), device_id_type=MESH)

    def z_rows(k):
        return pos(k) // z_part, pl.ds(pos(k) % z_part * owned, owned)

    def gz_copy(h, k):
        q, at = z_rows(0)
        to_q, to_at = z_rows((n_z - k) % n_z)
        return pltpu.make_async_remote_copy(
            src_ref=table.at[h, q, 0, at], dst_ref=table.at[h, to_q, 0, to_at], send_sem=gz_s,
            recv_sem=gz_r.at[h, to_q], device_id=(grp_z(k), m), device_id_type=MESH)

    def gx_copy(h, q, j):
        return pltpu.make_async_remote_copy(
            src_ref=table.at[h, q, 0], dst_ref=table.at[h, q, NX - j], send_sem=gx_s.at[h], recv_sem=gx_r.at[h],
            device_id=(grp_x(j), m), device_id_type=MESH)

    def b_copy(h, dy, dc):
        to = mem_of(-dy, dc)
        return pltpu.make_async_remote_copy(
            src_ref=served.at[h, pl.ds(slot_of(dy, dc) * slots, slots)],
            dst_ref=mirror.at[pl.ds(pl.multiple_of(m * slots, slots), slots), pl.ds(h * LANE, LANE)],
            send_sem=b_s.at[h], recv_sem=b_r.at[h], device_id=(g, to), device_id_type=MESH)

    def tell(r):
        if r < half_z - 1:
            pl.semaphore_signal(up_s.at[r], inc=1, device_id=(grp_z(1), m), device_id_type=MESH)
            pl.semaphore_signal(down_s.at[r], inc=1, device_id=(grp_z(n_z - 1), m), device_id_type=MESH)

    def hear(r):
        pl.semaphore_wait(up_s.at[r], 1)
        pl.semaphore_wait(down_s.at[r], 1)
        tell(r + 1)

    def drain(ref, sem):
        pltpu.make_async_copy(ref, ref, sem).wait()

    mine = pl.ds(pl.multiple_of(m * slots, slots), slots)
    for h in range(HALVES):
        if h:
            fill_rhs(h)
        for i, dy in enumerate(reversed(y_order)):
            sums_for(h, dy)
            if h == 0 and i == 0:
                pl.semaphore_wait(barrier, len(partners))
            for dc in range(NC):
                if (dy, dc) in mem_order and not (h and dy in near):
                    y_copy(h, dy, dc).start()
            if h == 0 and i == 0:
                tell(0)
            if h == 0 and i == 2:
                find_places()
                for d in mem_order:
                    id_copy(*d).start()
        precv[h, 0:slots] = part[h, 0, pl.ds(pl.multiple_of(c * slots, slots), slots), :]

    hear(0)
    drain(idrecv.at[pl.ds(1, n_mem - 1)], id_r)
    idrecv[0] = place[y]
    for k in range(n_y):
        even[k : k + 1, :] = idrecv[NC * k]
        odd[k : k + 1, :] = idrecv[NC * k + 1]
    lane = lax.broadcasted_iota(jnp.int32, (n_y, LANE), 1)
    low = jnp.where(c == 0, even[...], pltpu.roll(even[...], slots, 1))
    high = jnp.where(c == 0, pltpu.roll(odd[...], slots, 1), odd[...])
    spot = jnp.where(lane < slots, low, high)
    n_table = PARTS * NX * rows
    even[...] = spot

    def build_put(v, carry):
        row = lax.broadcasted_iota(jnp.int32, (LANE, LANE), 0) + v * LANE
        for k in range(n_y):
            put[pl.ds(pl.multiple_of(v * LANE, LANE), LANE), k * LANE : (k + 1) * LANE] = jnp.where(
                row == even[k : k + 1, :], 1.0, 0.0).astype(jnp.bfloat16)
        return carry

    lax.fori_loop(0, n_table // LANE, build_put, 0)

    hear(1)

    def rest_of_x(h, first, last):
        for q in range(first, last):
            drain(xrecv.at[h, q, pl.ds(1, NX - 1)], x_r.at[h, q])
            total = xacc[h, q]
            for j in range(1, NX):
                total = total + xrecv[h, q, j].astype(jnp.float32)
            xacc[h, q] = total
            for i in range(z_part):
                zsend[h, q * z_part + i] = total[i * owned : (i + 1) * owned].astype(jnp.bfloat16)
            for k in z_order:
                if pos(k) // z_part == q:
                    z_copy(h, k).start()

    group_rows = NX * rows
    for h in range(HALVES):
        drain(precv.at[h, pl.ds(slots, slot_total - slots)], y_r.at[h])
        if h == 0:
            for d in mem_order:
                if d[0] in near:
                    y_copy(1, *d).start()
        for q in range(PARTS):
            block = jnp.dot(put[q * group_rows : (q + 1) * group_rows, :], precv[h], preferred_element_type=jnp.float32)
            for j in x_order:
                col[h, q, j] = block[j * rows : (j + 1) * rows].astype(jnp.bfloat16)
                x_copy(h, q, j).start()
            xacc[h, q] = block[0:rows]
        if h == 0:
            for r in range(2, half_z - 1):
                hear(r)
            rest_of_x(0, 0, PARTS // 3)

    rest_of_x(0, PARTS // 3, PARTS)
    rest_of_x(1, 0, PARTS)

    def build_take(k, carry):
        column = jnp.broadcast_to(even[pl.ds(k, 1), :], (LANE, LANE)).T
        for v in range(n_table // LANE):
            row = lax.broadcasted_iota(jnp.int32, (LANE, LANE), 1) + v * LANE
            take[pl.ds(pl.multiple_of(k * LANE, LANE), LANE), v * LANE : (v + 1) * LANE] = jnp.where(
                column == row, 1.0, 0.0).astype(jnp.bfloat16)
        return carry

    lax.fori_loop(0, n_y, build_take, 0)
    for copy in fetch[5:]:
        copy.wait()
    drain(idrecv.at[pl.ds(1, n_mem - 1)], id_s)
    for h in range(HALVES):
        drain(precv.at[h, pl.ds(slots, slot_total - slots)], y_s.at[h])
        drain(xrecv.at[h, :, pl.ds(1, NX - 1)], x_s.at[h])

    own_q, own_at = z_rows(0)
    sums = []
    for h in range(HALVES):
        drain(zrecv.at[h, pl.ds(1, n_z - 1)], z_r.at[h])
        total = xacc[h, own_q, own_at, :]
        for k in range(1, n_z):
            total = total + zrecv[h, k].astype(jnp.float32)
        sums.append(total)

    scale = lax.rsqrt(mdeg[...].astype(jnp.float32))
    diagonal = lax.broadcasted_iota(jnp.int32, (owned, owned), 0) == lax.broadcasted_iota(
        jnp.int32, (owned, owned), 1)
    scale = jnp.sum(jnp.where(diagonal, jnp.broadcast_to(scale, (owned, owned)), 0.0), axis=1, keepdims=True)
    neigh = jnp.concatenate(sums, axis=1) * scale
    embed = mrow[...].astype(jnp.float32)
    first = (embed + neigh).astype(jnp.bfloat16)
    second = (neigh * embed).astype(jnp.bfloat16)
    result = jnp.dot(first, w1[...], preferred_element_type=jnp.float32) + jnp.dot(
        second, w2[...], preferred_element_type=jnp.float32)
    new = jnp.where(result > 0, result, 0.2 * result).astype(jnp.bfloat16)
    for h in range(HALVES):
        table[h, own_q, 0, own_at, :] = new[:, h * LANE : (h + 1) * LANE]

    for k in z_order[:3] + z_order[:2:-1]:
        gz_copy(0, k).start()
    newm[...] = new
    for h in range(HALVES):
        for q in reversed(range(PARTS)):
            n_here = z_part - (1 if q == own_q else 0)
            drain(table.at[h, q, 0, pl.ds(0, n_here * owned)], gz_r.at[h, q])
            for j in x_order:
                gx_copy(h, q, j).start()
            if (h, q) == (0, PARTS // 2):
                for k in reversed(z_order):
                    gz_copy(1, k).start()

    for h in range(HALVES):
        drain(table.at[h, :, pl.ds(1, NX - 1)], gx_r.at[h])
        for first in (4, 2, 6, 0):
            at = slice(first * LANE, (first + 2) * LANE)
            served[h, at, :] = jnp.dot(
                take[at, :], table[h].reshape(n_table, LANE), preferred_element_type=jnp.float32
            ).astype(jnp.bfloat16)
            for d in mem_order:
                if d[0] // 2 * 2 == first and d[0] not in near:
                    b_copy(h, *d).start()
        mirror[mine, h * LANE : (h + 1) * LANE] = served[h, 0:slots, :]

    for h in range(HALVES):
        for d in mem_order:
            if d[0] in near:
                b_copy(h, *d).start()

    drain(zrecv.at[:, pl.ds(1, n_z - 1)], gz_s)
    for h in range(HALVES):
        drain(zrecv.at[h, pl.ds(1, n_z - 1)], z_s.at[h])
        drain(table.at[h, :, pl.ds(1, NX - 1)], gx_s.at[h])
    for h in range(HALVES):
        drain(served.at[h, pl.ds(slots, slot_total - slots)], b_s.at[h])
        drain(served.at[h, pl.ds(slots, slot_total - slots)], b_r.at[h])


def hand_over(new_in, mirror_in, new_out, mirror_out, sems):
    copies = [
        pltpu.make_async_copy(mirror_in, mirror_out, sems.at[0]),
        pltpu.make_async_copy(new_in, new_out, sems.at[1]),
    ]
    for copy in copies:
        copy.start()
    for copy in copies:
        copy.wait()


def body(n_grp, n_mem, source_rows, source_degree, edge_tiles, tile_row, tile_col, mirror_ids,
         master_rows, master_degree, weight_one, weight_two):
    n_tiles, tile, _ = edge_tiles.shape
    src_dev, width = source_rows.shape
    slot_total = mirror_ids.shape[0]
    owned = master_rows.shape[0]
    n_z = n_grp // NX
    z_part = n_z // PARTS
    rows = z_part * owned
    n_table = n_z * NX * owned
    hbm = pl.BlockSpec(memory_space=pltpu.HBM)
    vmem = pl.BlockSpec(memory_space=pltpu.VMEM)
    bf, f32, i32 = jnp.bfloat16, jnp.float32, jnp.int32
    dma = pltpu.SemaphoreType.DMA
    operands = (
        tile_row, tile_col, source_rows, source_degree.reshape(-1, tile), edge_tiles, mirror_ids.reshape(-1, LANE),
        master_rows, master_degree.reshape(1, owned), weight_one, weight_two,
    )
    operands = [pltpu.with_memory_space_constraint(a, pltpu.HBM) for a in operands]
    outs = pl.pallas_call(
        functools.partial(kernel, n_grp, n_mem),
        out_shape=(
            pltpu.VMEM((owned, width), bf),
            pltpu.VMEM((slot_total, width), bf),
        ),
        in_specs=[hbm] * len(operands),
        out_specs=(vmem, vmem),
        scratch_shapes=[
            pltpu.SMEM((n_tiles,), i32),
            pltpu.SMEM((n_tiles,), i32),
            pltpu.VMEM((src_dev, width), bf),
            pltpu.VMEM((src_dev // tile, tile), i32),
            pltpu.VMEM((n_tiles, tile, tile), i32),
            pltpu.VMEM((slot_total // LANE, LANE), i32),
            pltpu.VMEM((owned, width), bf),
            pltpu.VMEM((1, owned), i32),
            pltpu.VMEM((width, width), bf),
            pltpu.VMEM((width, width), bf),
            pltpu.VMEM((HALVES, src_dev // tile, tile, LANE), bf),
            pltpu.VMEM((n_tiles, tile, tile), bf),
            pltpu.VMEM((n_mem // NC, tile, n_tiles * tile), bf),
            pltpu.VMEM((HALVES, n_tiles * tile, LANE), bf),
            pltpu.VMEM((HALVES, n_mem // NC, tile, LANE), bf),
            pltpu.VMEM((n_mem // NC, 1, LANE), i32),
            pltpu.VMEM((n_mem, 1, LANE), i32),
            pltpu.VMEM((slot_total // LANE, LANE), i32),
            pltpu.VMEM((slot_total // LANE, LANE), i32),
            pltpu.VMEM((n_table, slot_total), bf),
            pltpu.VMEM((slot_total, n_table), bf),
            pltpu.VMEM((HALVES, slot_total, LANE), bf),
            pltpu.VMEM((HALVES, PARTS, NX, rows, LANE), bf),
            pltpu.VMEM((HALVES, PARTS, rows, LANE), f32),
            pltpu.VMEM((HALVES, PARTS, NX, rows, LANE), bf),
            pltpu.VMEM((HALVES, n_z, owned, LANE), bf),
            pltpu.VMEM((HALVES, n_z, owned, LANE), bf),
            pltpu.VMEM((HALVES, PARTS, NX, rows, LANE), bf),
            pltpu.VMEM((HALVES, slot_total, LANE), bf),
            pltpu.SemaphoreType.REGULAR((n_z // 2 - 1,)), pltpu.SemaphoreType.REGULAR((n_z // 2 - 1,)),
            dma((len(operands) - 1,)), dma((FETCH,)),
            dma, dma,
            dma((HALVES,)), dma((HALVES,)),
            dma((HALVES,)), dma((HALVES, PARTS)),
            dma((HALVES,)), dma((HALVES,)),
            dma, dma((HALVES, PARTS)),
            dma((HALVES,)), dma((HALVES,)),
            dma((HALVES,)), dma((HALVES,)),
        ],
        compiler_params=pltpu.CompilerParams(
            collective_id=0, has_side_effects=True, vmem_limit_bytes=40 * 2**20),
        name="layer",
    )(*operands)
    return pl.pallas_call(
        hand_over,
        out_shape=tuple(jax.ShapeDtypeStruct(o.shape, o.dtype) for o in outs),
        in_specs=[vmem, vmem],
        out_specs=(hbm, hbm),
        scratch_shapes=[dma((2,))],
        compiler_params=pltpu.CompilerParams(vmem_limit_bytes=16 * 2**20),
        name="hand_over",
    )(*outs)


def solution(mesh):
    both = ("grp", "mem")
    in_specs = (
        P(both, None), P(both), P(both, None, None), P(both), P(both), P(both),
        P(both, None), P(both), P(), P(),
    )
    out_specs = (P(both, None), P(both, None))
    fn = functools.partial(body, mesh.shape["grp"], mesh.shape["mem"])
    return jax.shard_map(fn, mesh=mesh, in_specs=in_specs, out_specs=out_specs, check_vma=False)
```

```python
import functools

import jax
import jax.numpy as jnp
from jax import lax
from jax.experimental import pallas as pl
from jax.experimental.pallas import tpu as pltpu
from jax.sharding import PartitionSpec as P

MESH = pl.DeviceIdType.MESH
NX = 4
NC = 2
LANE = 128
HALVES = 2
PARTS = 6
FETCH = 4


def log2(n):
    assert n & (n - 1) == 0
    return n.bit_length() - 1


def kernel(
    n_grp, n_mem, trow_h, tcol_h, src_h, deg_h, tiles_h, ids_h, mrow_h, mdeg_h, w1_h, w2_h, newm, mirror,
    trow, tcol, src, deg, tiles, idin, mrow, mdeg, w1, w2,
    scaled, bits, lhs, rhs, part, place, idrecv, even, odd, put, take, precv, col, xacc, xrecv, zsend, zrecv, table, served,
    up_s, down_s, in_s, tile_s, id_s, id_r, y_s, y_r, x_s, x_r, z_s, z_r, gz_s, gz_r, gx_s, gx_r, b_s, b_r,
):
    g = lax.axis_index("grp")
    m = lax.axis_index("mem")
    n_z, n_y = n_grp // NX, n_mem // NC
    x, z = lax.rem(g, NX), g // NX
    c, y = lax.rem(m, NC), m // NC
    tile = tiles.shape[1]
    n_tiles = tiles.shape[0]
    slot_total = precv.shape[1]
    slots = slot_total // n_mem
    owned = mrow.shape[0]
    half_z = n_z // 2
    z_part = n_z // PARTS
    rows = z_part * owned

    def mem_of(dy, dc):
        return lax.rem(y + dy + n_y, n_y) * NC + lax.rem(c + dc, NC)

    def grp_x(j):
        return z * NX + lax.rem(x + j + NX, NX)

    def grp_z(k):
        return lax.rem(z + k + n_z, n_z) * NX + x

    def pos(k):
        return 2 * abs(k - half_z) - (1 if k < half_z else 0)

    y_order = [0] + [s for d in range(1, n_y // 2) for s in (n_y - d, d)] + [n_y // 2]
    mem_order = [(dy, dc) for dy in reversed(y_order) for dc in range(NC) if (dy, dc) != (0, 0)]
    near = (1, n_y - 1, 0)
    x_order = sorted(range(1, NX), key=lambda j: -min(j, NX - j))
    z_order = sorted(range(1, n_z), key=pos)

    fetch = [
        pltpu.make_async_copy(a, b, in_s.at[i])
        for i, (a, b) in enumerate([
            (deg_h, deg), (src_h, src), (trow_h, trow), (tcol_h, tcol), (ids_h, idin),
            (mrow_h, mrow), (mdeg_h, mdeg), (w1_h, w1), (w2_h, w2)])
    ]
    step = n_tiles // FETCH
    fetch_tiles = [
        pltpu.make_async_copy(tiles_h.at[pl.ds(i * step, step)], tiles.at[pl.ds(i * step, step)], tile_s.at[i])
        for i in range(FETCH)
    ]
    barrier = pltpu.get_barrier_semaphore()
    partners = [(g, mem_of(*d)) for d in mem_order] + [(grp_x(j), m) for j in x_order] + [
        (grp_z(k), m) for k in (1, n_z - 1)]
    def greet(some):
        for who in some:
            pl.semaphore_signal(barrier, inc=1, device_id=who, device_id_type=MESH)

    far = NC * (n_y // 2 - 1)
    greet(partners[:far])
    for copy in fetch[:2] + fetch_tiles + fetch[2:5]:
        copy.start()
    greet(partners[far:])
    for copy in fetch[5:]:
        copy.start()

    fetch[0].wait()
    fetch[1].wait()
    scale = lax.rsqrt(deg[...].astype(jnp.float32))
    columns = [
        jnp.broadcast_to(scale[k : k + 1, :], (tile, tile)).T for k in range(src.shape[0] // tile)]
    for copy in fetch[2:5]:
        copy.wait()

    def fill_rhs(h):
        for k, column in enumerate(columns):
            at = (pl.ds(k * tile, tile), pl.ds(h * LANE, LANE))
            scaled[h, k] = (src[at].astype(jnp.float32) * column).astype(jnp.bfloat16)
        for t in range(n_tiles):
            rhs[h, t * tile : (t + 1) * tile, :] = scaled[h, tcol[t]]

    def fill_lhs(dy, tiles_here):
        block = lax.rem(y + dy, n_y)
        for t in tiles_here:
            edges = bits[t]
            lhs[dy, :, t * tile : (t + 1) * tile] = jnp.where(trow[t] == block, edges, jnp.zeros_like(edges))

    fill_rhs(0)
    farthest, total = y_order[-1], None
    for i in range(FETCH):
        fetch_tiles[i].wait()
        here = range(i * step, (i + 1) * step)
        for t in here:
            bits[t] = tiles[t].astype(jnp.float32).astype(jnp.bfloat16)
        fill_lhs(farthest, here)
        deep = slice(i * step * tile, (i + 1) * step * tile)
        product = jnp.dot(lhs[farthest, :, deep], rhs[0, deep], preferred_element_type=jnp.float32)
        total = product if total is None else total + product
    part[0, farthest] = total.astype(jnp.bfloat16)

    def find_places():
        ids = idin[...]
        group = jnp.right_shift(ids, log2(owned * n_mem))
        dx = jnp.bitwise_and(group, NX - 1) - x
        dx = jnp.where(dx < 0, dx + NX, dx)
        dz = jnp.right_shift(group, log2(NX)) - z
        dz = jnp.where(dz < 0, dz + n_z, dz)
        order = 2 * jnp.abs(dz - half_z) - jnp.where(dz < half_z, 1, 0)
        z_group = jnp.right_shift(order, log2(z_part))
        spots = (z_group * NX + dx) * rows + jnp.bitwise_and(order, z_part - 1) * owned + jnp.bitwise_and(
            ids, owned - 1)

        for k in range(n_y):
            place[k] = spots[k : k + 1, :]

    def sums_for(h, dy):
        if (h, dy) != (0, farthest):
            if h == 0:
                fill_lhs(dy, range(n_tiles))
            part[h, dy] = jnp.dot(lhs[dy], rhs[h], preferred_element_type=jnp.float32).astype(jnp.bfloat16)

    def slot_of(dy, dc):
        return dy * NC + dc

    def id_copy(dy, dc):
        return pltpu.make_async_remote_copy(
            src_ref=place.at[lax.rem(y + dy, n_y)], dst_ref=idrecv.at[slot_of(dy, dc)], send_sem=id_s, recv_sem=id_r,
            device_id=(g, mem_of(dy, dc)), device_id_type=MESH)

    def y_copy(h, dy, dc):
        to = mem_of(dy, dc)
        return pltpu.make_async_remote_copy(
            src_ref=part.at[h, dy, pl.ds(pl.multiple_of(lax.rem(to, NC) * slots, slots), slots)],
            dst_ref=precv.at[h, pl.ds(slot_of(dy, dc) * slots, slots)],
            send_sem=y_s.at[h], recv_sem=y_r.at[h], device_id=(g, to), device_id_type=MESH)

    def x_copy(h, q, j):
        return pltpu.make_async_remote_copy(
            src_ref=col.at[h, q, j], dst_ref=xrecv.at[h, q, j], send_sem=x_s.at[h], recv_sem=x_r.at[h, q],
            device_id=(grp_x(j), m), device_id_type=MESH)

    def z_copy(h, k):
        return pltpu.make_async_remote_copy(
            src_ref=zsend.at[h, pos(k)], dst_ref=zrecv.at[h, k], send_sem=z_s.at[h], recv_sem=z_r.at[h],
            device_id=(grp_z(k), m), device_id_type=MESH)

    def z_rows(k):
        return pos(k) // z_part, pl.ds(pos(k) % z_part * owned, owned)

    def gz_copy(h, k):
        q, at = z_rows(0)
        to_q, to_at = z_rows((n_z - k) % n_z)
        return pltpu.make_async_remote_copy(
            src_ref=table.at[h, q, 0, at], dst_ref=table.at[h, to_q, 0, to_at], send_sem=gz_s,
            recv_sem=gz_r.at[h, to_q], device_id=(grp_z(k), m), device_id_type=MESH)

    def gx_copy(h, q, j):
        return pltpu.make_async_remote_copy(
            src_ref=table.at[h, q, 0], dst_ref=table.at[h, q, NX - j], send_sem=gx_s.at[h], recv_sem=gx_r.at[h],
            device_id=(grp_x(j), m), device_id_type=MESH)

    def b_copy(h, dy, dc):
        to = mem_of(-dy, dc)
        return pltpu.make_async_remote_copy(
            src_ref=served.at[h, pl.ds(slot_of(dy, dc) * slots, slots)],
            dst_ref=mirror.at[pl.ds(pl.multiple_of(m * slots, slots), slots), pl.ds(h * LANE, LANE)],
            send_sem=b_s.at[h], recv_sem=b_r.at[h], device_id=(g, to), device_id_type=MESH)

    def tell(r):
        if r < half_z - 1:
            pl.semaphore_signal(up_s.at[r], inc=1, device_id=(grp_z(1), m), device_id_type=MESH)
            pl.semaphore_signal(down_s.at[r], inc=1, device_id=(grp_z(n_z - 1), m), device_id_type=MESH)

    def hear(r):
        pl.semaphore_wait(up_s.at[r], 1)
        pl.semaphore_wait(down_s.at[r], 1)
        tell(r + 1)

    def drain(ref, sem):
        pltpu.make_async_copy(ref, ref, sem).wait()

    mine = pl.ds(pl.multiple_of(m * slots, slots), slots)
    for h in range(HALVES):
        if h:
            fill_rhs(h)
        for i, dy in enumerate(reversed(y_order)):
            sums_for(h, dy)
            if h == 0 and i == 0:
                pl.semaphore_wait(barrier, len(partners))
            for dc in range(NC):
                if (dy, dc) in mem_order and not (h and dy in near):
                    y_copy(h, dy, dc).start()
            if h == 0 and i == 0:
                tell(0)
            if h == 0 and i == 2:
                find_places()
                for d in mem_order:
                    id_copy(*d).start()
        precv[h, 0:slots] = part[h, 0, pl.ds(pl.multiple_of(c * slots, slots), slots), :]

    hear(0)
    drain(idrecv.at[pl.ds(1, n_mem - 1)], id_r)
    idrecv[0] = place[y]
    for k in range(n_y):
        even[k : k + 1, :] = idrecv[NC * k]
        odd[k : k + 1, :] = idrecv[NC * k + 1]
    lane = lax.broadcasted_iota(jnp.int32, (n_y, LANE), 1)
    low = jnp.where(c == 0, even[...], pltpu.roll(even[...], slots, 1))
    high = jnp.where(c == 0, pltpu.roll(odd[...], slots, 1), odd[...])
    spot = jnp.where(lane < slots, low, high)
    n_table = PARTS * NX * rows
    even[...] = spot

    def build_put(v, carry):
        row = lax.broadcasted_iota(jnp.int32, (LANE, LANE), 0) + v * LANE
        for k in range(n_y):
            put[pl.ds(pl.multiple_of(v * LANE, LANE), LANE), k * LANE : (k + 1) * LANE] = jnp.where(
                row == even[k : k + 1, :], 1.0, 0.0).astype(jnp.bfloat16)
        return carry

    lax.fori_loop(0, n_table // LANE, build_put, 0)

    hear(1)

    def rest_of_x(h, first, last):
        for q in range(first, last):
            drain(xrecv.at[h, q, pl.ds(1, NX - 1)], x_r.at[h, q])
            total = xacc[h, q]
            for j in range(1, NX):
                total = total + xrecv[h, q, j].astype(jnp.float32)
            xacc[h, q] = total
            for i in range(z_part):
                zsend[h, q * z_part + i] = total[i * owned : (i + 1) * owned].astype(jnp.bfloat16)
            for k in z_order:
                if pos(k) // z_part == q:
                    z_copy(h, k).start()

    group_rows = NX * rows
    for h in range(HALVES):
        drain(precv.at[h, pl.ds(slots, slot_total - slots)], y_r.at[h])
        if h == 0:
            for d in mem_order:
                if d[0] in near:
                    y_copy(1, *d).start()
        for q in range(PARTS):
            block = jnp.dot(put[q * group_rows : (q + 1) * group_rows, :], precv[h], preferred_element_type=jnp.float32)
            for j in x_order:
                col[h, q, j] = block[j * rows : (j + 1) * rows].astype(jnp.bfloat16)
                x_copy(h, q, j).start()
            xacc[h, q] = block[0:rows]
        if h == 0:
            for r in range(2, half_z - 1):
                hear(r)
            rest_of_x(0, 0, PARTS // 3)

    rest_of_x(0, PARTS // 3, PARTS)
    rest_of_x(1, 0, PARTS)

    def build_take(k, carry):
        column = jnp.broadcast_to(even[pl.ds(k, 1), :], (LANE, LANE)).T
        for v in range(n_table // LANE):
            row = lax.broadcasted_iota(jnp.int32, (LANE, LANE), 1) + v * LANE
            take[pl.ds(pl.multiple_of(k * LANE, LANE), LANE), v * LANE : (v + 1) * LANE] = jnp.where(
                column == row, 1.0, 0.0).astype(jnp.bfloat16)
        return carry

    lax.fori_loop(0, n_y, build_take, 0)
    for copy in fetch[5:]:
        copy.wait()
    drain(idrecv.at[pl.ds(1, n_mem - 1)], id_s)
    for h in range(HALVES):
        drain(precv.at[h, pl.ds(slots, slot_total - slots)], y_s.at[h])
        drain(xrecv.at[h, :, pl.ds(1, NX - 1)], x_s.at[h])

    own_q, own_at = z_rows(0)
    sums = []
    for h in range(HALVES):
        drain(zrecv.at[h, pl.ds(1, n_z - 1)], z_r.at[h])
        total = xacc[h, own_q, own_at, :]
        for k in range(1, n_z):
            total = total + zrecv[h, k].astype(jnp.float32)
        sums.append(total)

    scale = lax.rsqrt(mdeg[...].astype(jnp.float32))
    diagonal = lax.broadcasted_iota(jnp.int32, (owned, owned), 0) == lax.broadcasted_iota(
        jnp.int32, (owned, owned), 1)
    scale = jnp.sum(jnp.where(diagonal, jnp.broadcast_to(scale, (owned, owned)), 0.0), axis=1, keepdims=True)
    neigh = jnp.concatenate(sums, axis=1) * scale
    embed = mrow[...].astype(jnp.float32)
    first = (embed + neigh).astype(jnp.bfloat16)
    second = (neigh * embed).astype(jnp.bfloat16)
    result = jnp.dot(first, w1[...], preferred_element_type=jnp.float32) + jnp.dot(
        second, w2[...], preferred_element_type=jnp.float32)
    new = jnp.where(result > 0, result, 0.2 * result).astype(jnp.bfloat16)
    for h in range(HALVES):
        table[h, own_q, 0, own_at, :] = new[:, h * LANE : (h + 1) * LANE]

    for k in z_order[:3] + z_order[:2:-1]:
        gz_copy(0, k).start()
    newm[...] = new
    for h in range(HALVES):
        for q in reversed(range(PARTS)):
            n_here = z_part - (1 if q == own_q else 0)
            drain(table.at[h, q, 0, pl.ds(0, n_here * owned)], gz_r.at[h, q])
            for j in x_order:
                gx_copy(h, q, j).start()
            if (h, q) == (0, PARTS // 2):
                for k in reversed(z_order):
                    gz_copy(1, k).start()

    for h in range(HALVES):
        drain(table.at[h, :, pl.ds(1, NX - 1)], gx_r.at[h])
        for first in (4, 2, 6, 0):
            at = slice(first * LANE, (first + 2) * LANE)
            served[h, at, :] = jnp.dot(
                take[at, :], table[h].reshape(n_table, LANE), preferred_element_type=jnp.float32
            ).astype(jnp.bfloat16)
            for d in mem_order:
                if d[0] // 2 * 2 == first and d[0] not in near:
                    b_copy(h, *d).start()
        mirror[mine, h * LANE : (h + 1) * LANE] = served[h, 0:slots, :]

    for h in range(HALVES):
        for d in mem_order:
            if d[0] in near:
                b_copy(h, *d).start()

    drain(zrecv.at[:, pl.ds(1, n_z - 1)], gz_s)
    for h in range(HALVES):
        drain(zrecv.at[h, pl.ds(1, n_z - 1)], z_s.at[h])
        drain(table.at[h, :, pl.ds(1, NX - 1)], gx_s.at[h])
    for h in range(HALVES):
        drain(served.at[h, pl.ds(slots, slot_total - slots)], b_s.at[h])
        drain(served.at[h, pl.ds(slots, slot_total - slots)], b_r.at[h])


def hand_over(new_in, mirror_in, new_out, mirror_out, sems):
    copies = [
        pltpu.make_async_copy(mirror_in, mirror_out, sems.at[0]),
        pltpu.make_async_copy(new_in, new_out, sems.at[1]),
    ]
    for copy in copies:
        copy.start()
    for copy in copies:
        copy.wait()


def body(n_grp, n_mem, source_rows, source_degree, edge_tiles, tile_row, tile_col, mirror_ids,
         master_rows, master_degree, weight_one, weight_two):
    n_tiles, tile, _ = edge_tiles.shape
    src_dev, width = source_rows.shape
    slot_total = mirror_ids.shape[0]
    owned = master_rows.shape[0]
    n_z = n_grp // NX
    z_part = n_z // PARTS
    rows = z_part * owned
    n_table = n_z * NX * owned
    hbm = pl.BlockSpec(memory_space=pltpu.HBM)
    vmem = pl.BlockSpec(memory_space=pltpu.VMEM)
    bf, f32, i32 = jnp.bfloat16, jnp.float32, jnp.int32
    dma = pltpu.SemaphoreType.DMA
    operands = (
        tile_row, tile_col, source_rows, source_degree.reshape(-1, tile), edge_tiles, mirror_ids.reshape(-1, LANE),
        master_rows, master_degree.reshape(1, owned), weight_one, weight_two,
    )
    operands = [pltpu.with_memory_space_constraint(a, pltpu.HBM) for a in operands]
    outs = pl.pallas_call(
        functools.partial(kernel, n_grp, n_mem),
        out_shape=(
            pltpu.VMEM((owned, width), bf),
            pltpu.VMEM((slot_total, width), bf),
        ),
        in_specs=[hbm] * len(operands),
        out_specs=(vmem, vmem),
        scratch_shapes=[
            pltpu.SMEM((n_tiles,), i32),
            pltpu.SMEM((n_tiles,), i32),
            pltpu.VMEM((src_dev, width), bf),
            pltpu.VMEM((src_dev // tile, tile), i32),
            pltpu.VMEM((n_tiles, tile, tile), i32),
            pltpu.VMEM((slot_total // LANE, LANE), i32),
            pltpu.VMEM((owned, width), bf),
            pltpu.VMEM((1, owned), i32),
            pltpu.VMEM((width, width), bf),
            pltpu.VMEM((width, width), bf),
            pltpu.VMEM((HALVES, src_dev // tile, tile, LANE), bf),
            pltpu.VMEM((n_tiles, tile, tile), bf),
            pltpu.VMEM((n_mem // NC, tile, n_tiles * tile), bf),
            pltpu.VMEM((HALVES, n_tiles * tile, LANE), bf),
            pltpu.VMEM((HALVES, n_mem // NC, tile, LANE), bf),
            pltpu.VMEM((n_mem // NC, 1, LANE), i32),
            pltpu.VMEM((n_mem, 1, LANE), i32),
            pltpu.VMEM((slot_total // LANE, LANE), i32),
            pltpu.VMEM((slot_total // LANE, LANE), i32),
            pltpu.VMEM((n_table, slot_total), bf),
            pltpu.VMEM((slot_total, n_table), bf),
            pltpu.VMEM((HALVES, slot_total, LANE), bf),
            pltpu.VMEM((HALVES, PARTS, NX, rows, LANE), bf),
            pltpu.VMEM((HALVES, PARTS, rows, LANE), f32),
            pltpu.VMEM((HALVES, PARTS, NX, rows, LANE), bf),
            pltpu.VMEM((HALVES, n_z, owned, LANE), bf),
            pltpu.VMEM((HALVES, n_z, owned, LANE), bf),
            pltpu.VMEM((HALVES, PARTS, NX, rows, LANE), bf),
            pltpu.VMEM((HALVES, slot_total, LANE), bf),
            pltpu.SemaphoreType.REGULAR((n_z // 2 - 1,)), pltpu.SemaphoreType.REGULAR((n_z // 2 - 1,)),
            dma((len(operands) - 1,)), dma((FETCH,)),
            dma, dma,
            dma((HALVES,)), dma((HALVES,)),
            dma((HALVES,)), dma((HALVES, PARTS)),
            dma((HALVES,)), dma((HALVES,)),
            dma, dma((HALVES, PARTS)),
            dma((HALVES,)), dma((HALVES,)),
            dma((HALVES,)), dma((HALVES,)),
        ],
        compiler_params=pltpu.CompilerParams(
            collective_id=0, has_side_effects=True, vmem_limit_bytes=40 * 2**20),
        name="layer",
    )(*operands)
    return pl.pallas_call(
        hand_over,
        out_shape=tuple(jax.ShapeDtypeStruct(o.shape, o.dtype) for o in outs),
        in_specs=[vmem, vmem],
        out_specs=(hbm, hbm),
        scratch_shapes=[dma((2,))],
        compiler_params=pltpu.CompilerParams(vmem_limit_bytes=16 * 2**20),
        name="hand_over",
    )(*outs)


def solution(mesh):
    both = ("grp", "mem")
    in_specs = (
        P(both, None), P(both), P(both, None, None), P(both), P(both), P(both),
        P(both, None), P(both), P(), P(),
    )
    out_specs = (P(both, None), P(both, None))
    fn = functools.partial(body, mesh.shape["grp"], mesh.shape["mem"])
    return jax.shard_map(fn, mesh=mesh, in_specs=in_specs, out_specs=out_specs, check_vma=False)
```
